128 devices in a mesh: tp: 8 (over z, x_hi), fsdp: 16 (over y, x_lo, core).
Axes of the slice: x: 4 (x_hi: 2, x_lo: 2; x = x_hi * 2 + x_lo), y: 4, z: 4, core: 2. Of those that a mesh axis runs over, the one named last changes fastest.
Arguments:
- t_hid: bfloat16 [8192, 16384], P('fsdp', 'tp'), may hold values from -400 to 400
- teacher_gain: float32 [16384], P('tp'), may hold values from 0.25 to 1.75
- proj: bfloat16 [16384, 4096], P('tp'), may hold values from -0.046875 to 0.046875
- owner: int32 [8192, 1], P('fsdp'), may hold values from 0 to 15; in each aligned block of 512 rows (0 to 511, 512 to 1023, ...) at most 48 rows name the same one
- seg_ids: int32 [16, 512], P('fsdp'), may hold values from 0 to 7, never falling along the last dimension, each value on 1 to 256 neighbouring positions
- student_ctx: bfloat16 [12288, 4096], P('fsdp'), may hold values from -6 to 6
- student_resid: bfloat16 [12288, 4096], P('fsdp', 'tp'), may hold values from -6 to 6
- w_out: bfloat16 [4096, 4096], P('fsdp', 'tp'), may hold values from -0.09375 to 0.09375
Outputs:
- loss: float32 [], replicated
- w_grad: bfloat16 [4096, 4096], P('fsdp', 'tp')
The draws below stay inside these ranges and needn't reach their ends.
Inputs may be any that keep to these rules, and one draw needn't show every extreme that they name: Within each slab's 512 rows no owner is named by more than 48 rows, a bound that some block reaches of them.
All inputs are finite; a program needn't handle non-finite values.
Results may differ from the reference program's by a relative error of at most 0.0059.
Values may be sent and summed in bfloat16 or wider, within the bound.
A program may use at most 128 MiB of HBM per device.

```python
import math
import jax
import jax.numpy as jnp
import numpy as np
from jax import lax

D_T = 16384
D_S = 4096
SLAB = 512
SEGS = 8
MOSTLEN = 256
CAP = 48
TOKENS = 8192
S_ROWS = 12288
N_FSDP = 16


def draw_t_hid(key, part):
    key = jax.random.fold_in(key, 7)
    key_rows, key_cols, key_base = jax.random.split(key, 3)
    rows = 10.0 ** jax.random.uniform(key_rows, (TOKENS, 1), jnp.float32)
    place = jnp.arange(D_T, dtype=jnp.float32) / D_T
    cols = 3.0 ** place * 10.0 ** jax.random.uniform(key_cols, (D_T,), jnp.float32, minval=-0.5, maxval=0.5)
    base = jax.random.truncated_normal(key_base, -4.0, 4.0, (TOKENS, D_T), jnp.float32)
    return (base * rows * cols[None, :]).astype(jnp.bfloat16)


def strengthened(entries, stream_key, source, target, blocks, factor):
    def block_of(position):
        return (jnp.arange(entries.shape[position]) // (entries.shape[position] // blocks)).reshape((-1,) + (1,) * (entries.ndim - 1 - position))

    one_side = jax.random.permutation(stream_key, blocks)[block_of(target)]
    second = (block_of(target) + blocks // 2) % blocks
    return jnp.where((block_of(source) == one_side) | (block_of(source) == second), factor * entries, entries)


def steps_of(rng, dims, shards, smallest, top_value):
    def one(axis_at, blocks):
        steps = jax.random.uniform(jax.random.fold_in(jax.random.fold_in(rng, 6), axis_at), (blocks,), jnp.float32, smallest / len(shards), top_value / len(shards))
        return jnp.repeat(jnp.exp(steps), dims[axis_at] // blocks).reshape((-1,) + (1,) * (len(dims) - axis_at - 1))

    factor_of = one(*shards[0])
    for cut in shards[1:]:
        factor_of = factor_of * one(*cut)
    return factor_of


def profile(number_of, total, limit, lean):
    loads = [(1 << 20) // math.isqrt(standing ** lean) + 1 for standing in range(2, number_of + 1)]
    spare, given = total - limit - (number_of - 1), [1] * (number_of - 1)
    while spare > 0:
        candidates = [i for i in range(number_of - 1) if given[i] < limit]
        whole, remaining = sum([loads[i] for i in candidates]), spare
        for i in candidates:
            addition = min(limit - given[i], max(1, remaining * loads[i] // whole), spare)
            given[i] = given[i] + addition
            spare = spare - addition
    return np.array([limit] + given)


def uneven(stream_key, count, total, bound, lean):
    if count == 2:
        one = jax.random.randint(stream_key, (), max(1, total - bound), min(bound, total - 1) + 1)
        return jnp.stack([one, total - one])
    tallies = jnp.asarray(profile(count, total, bound, lean), jnp.int32)
    couples = (count - 1) // 2
    donor, sink = tallies[1:1 + 2 * couples:2], tallies[2:2 + 2 * couples:2]
    room = jnp.minimum(donor - 1, bound - sink)
    passed = jax.random.randint(jax.random.fold_in(stream_key, 1), (couples,), 0, 1 << 20) % (room + 1)
    tallies = tallies.at[1:1 + 2 * couples:2].set(donor - passed).at[2:2 + 2 * couples:2].set(sink + passed)
    return tallies[jax.random.permutation(jax.random.fold_in(stream_key, 2), count)]


def assign_block(stream_key, own, number, rows, amount, top, bound, slope):
    sequence = jax.random.permutation(stream_key, amount)
    packed, common = portions_of(amount, rows * top, bound, slope, True), portions_of(amount, rows * top, bound, slope, False)
    places = jnp.arange(amount)

    def named(sizes, rotation):
        used = int((sizes > 0).sum())
        fixed = max(1, used // 4)
        moved = fixed + (places - fixed + rotation * (used - fixed)) % max(1, amount - fixed)
        return jnp.zeros((amount,), jnp.int32).at[sequence[jnp.where(places < fixed, places, moved)]].set(jnp.asarray(sizes, jnp.int32))

    sizes = jnp.where(number % 4 == 0, named(packed, number // 4), named(common, number - number // 4 - 1))
    mixed = jax.random.permutation(jax.random.fold_in(own, 3), amount)
    donor, taker = mixed[0:amount // 2 * 2:2], mixed[1:amount // 2 * 2:2]
    margin = jnp.minimum(sizes[donor] - 1, bound - sizes[taker]) // 2
    margin = jnp.where((donor == sequence[0]) | (taker == sequence[0]) | (sizes[taker] == 0), 0, jnp.maximum(margin, 0))
    moved = jax.random.randint(jax.random.fold_in(own, 4), (amount // 2,), 0, 1 << 20) % (margin + 1)
    sizes = sizes.at[donor].add(-moved).at[taker].add(moved)
    items = jnp.searchsorted(jnp.cumsum(sizes), jnp.arange(rows * top), side="right").astype(jnp.int32)
    listing = items.reshape(top, rows).T
    listing = listing[jax.random.permutation(jax.random.fold_in(own, 1), rows)]
    rotation = jax.random.randint(jax.random.fold_in(own, 2), (rows, 1), 0, top)
    return jnp.take_along_axis(listing, (jnp.arange(top)[None, :] + rotation) % top, axis=1)


def portions_of(amount, total, limit, skew, full):
    portions = [(1 << 20) // math.isqrt(grade ** skew) + 1 for grade in range(1, amount + 1)]
    largest = limit if full else min(limit, max(-(-total // amount), total * portions[0] // sum(portions)))
    least = 1 if total - largest >= amount - 1 else 0
    given, rest = [largest] + [least] * (amount - 1), total - largest - least * (amount - 1)
    while rest > 0:
        free = [i for i in range(1, amount) if given[i] < largest] or [i for i in range(1, amount) if given[i] < limit]
        pool, remaining = sum([portions[i] for i in free]), rest
        for i in free:
            extra = min(limit - given[i], max(1, remaining * portions[i] // pool), rest)
            given[i] = given[i] + extra
            rest = rest - extra
    return np.array(given)


def gaussian(key, shape, spread, reach, cuts=(), kind=jnp.bfloat16):
    factor_of = steps_of(key, shape, cuts, -0.22, 0.18) if cuts else 1.0
    result = jax.random.normal(key, shape, jnp.float32) * spread * factor_of
    return jnp.minimum(jnp.maximum(result, -reach), reach).astype(kind)


def heavy_noise(stream_key, extent, width, limit, shards, heavy, kind=jnp.bfloat16):
    values = width * jax.random.normal(stream_key, extent, jnp.float32)
    if shards:
        values = values * steps_of(stream_key, extent, shards, -0.22, 0.18)
    return jnp.clip(strengthened(values, jax.random.fold_in(stream_key, 3), *heavy), -limit, limit).astype(kind)


def setup_inputs(seed: int = 0) -> dict:
    key_list = jax.random.split(jax.random.key(seed), 9)
    t_hid = draw_t_hid(jax.random.fold_in(key_list[8], 71), 0)
    teacher_gain = jnp.clip(1.0 + 0.15 * jax.random.normal(key_list[1], (D_T,), jnp.float32), 0.25, 1.75)
    proj = gaussian(key_list[2], (D_T, D_S), D_T ** -0.5, 0.046875, ((0, 8),))
    owner_keys = jax.random.split(jax.random.fold_in(key_list[3], 1), TOKENS // SLAB)
    owner_turns = jax.random.permutation(jax.random.fold_in(key_list[3], 3), TOKENS // SLAB)
    owner = jax.vmap(lambda own, number: assign_block(jax.random.fold_in(key_list[3], 2), own, number, SLAB, N_FSDP, 1, CAP, 2))(owner_keys, owner_turns).reshape((TOKENS, 1))
    seg_ids = jax.vmap(lambda own: jnp.searchsorted(jnp.cumsum(uneven(own, SEGS, SLAB, MOSTLEN, 2)), jnp.arange(SLAB), side="right"))(jax.random.split(key_list[4], N_FSDP)).reshape((N_FSDP, SLAB)).astype(jnp.int32)
    student_ctx = heavy_noise(key_list[5], (S_ROWS, D_S), 1.0, 6.0, ((0, 16),), (0, 1, 16, 2.0))
    student_resid = gaussian(key_list[6], (S_ROWS, D_S), 1.0, 6.0, ((0, 16), (1, 8)))
    w_out = gaussian(key_list[7], (D_S, D_S), D_S ** -0.5, 0.09375, ((0, 16), (1, 8)))
    return {"t_hid": t_hid, "teacher_gain": teacher_gain, "proj": proj, "owner": owner, "seg_ids": seg_ids, "student_ctx": student_ctx, "student_resid": student_resid, "w_out": w_out}


def reference(t_hid, teacher_gain, proj, owner, seg_ids, student_ctx, student_resid, w_out):
    wide = t_hid.astype(jnp.float32)
    squares = lax.optimization_barrier(jnp.sum(wide * wide, axis=1))
    scale_rows = lax.rsqrt(squares / D_T + 1e-05)
    scaled = (wide * teacher_gain[None, :]).astype(jnp.bfloat16)
    raw = jnp.dot(scaled, proj, preferred_element_type=jnp.float32)
    fitted = (raw * scale_rows[:, None]).astype(jnp.bfloat16)
    member = (seg_ids[:, :, None] == jnp.arange(SEGS, dtype=jnp.int32)[None, None, :]).astype(jnp.int32)
    counts = lax.optimization_barrier(jnp.sum(member, axis=1))
    length = lax.optimization_barrier(jnp.sum(member * counts[:, None, :], axis=2))
    weight = (1.0 / length.astype(jnp.float32)).astype(jnp.bfloat16).reshape(TOKENS)
    dest = owner[:, 0].reshape(N_FSDP, SLAB)
    marks = (dest[:, :, None] == jnp.arange(N_FSDP, dtype=jnp.int32)[None, None, :]).astype(jnp.int32)
    before = jnp.cumsum(marks, axis=1) - marks
    rank = lax.optimization_barrier(jnp.sum(before * marks, axis=2))
    groups = jnp.arange(N_FSDP, dtype=jnp.int32)[:, None]
    slot = (dest * (N_FSDP * CAP) + groups * CAP + rank).reshape(TOKENS).astype(jnp.int32)
    targets = jnp.zeros((S_ROWS, D_S), jnp.bfloat16).at[slot].set(fitted)
    row_weight = jnp.zeros((S_ROWS,), jnp.bfloat16).at[slot].set(weight)
    hidden = student_resid.astype(jnp.float32) + jnp.dot(student_ctx, w_out, preferred_element_type=jnp.float32)
    diff = hidden - targets.astype(jnp.float32)
    weights = row_weight.astype(jnp.float32)
    denom = D_S * N_FSDP * SEGS
    loss = jnp.sum(weights * lax.optimization_barrier(jnp.sum(diff * diff, axis=1))) / denom
    grad_rows = (weights[:, None] * diff * (2.0 / denom)).astype(jnp.bfloat16)
    w_grad = lax.dot_general(student_ctx, grad_rows, (((0,), (0,)), ((), ())), preferred_element_type=jnp.float32)
    return (loss, w_grad.astype(jnp.bfloat16))
```

```python
import jax
import jax.numpy as jnp
from jax import lax
from jax.experimental import pallas as pl
from jax.experimental.pallas import tpu as pltpu
from jax.sharding import PartitionSpec as P

D_T = 16384
D_S = 4096
SEGS = 8
TP = 8
FS = 16
SLAB = 512
KT = D_T // TP
COLS = D_S // TP
CAP = 48
ROWS = FS * CAP
KB = D_S // FS
HALF = COLS // 2
LANES = 128
DENOM = D_S * FS * SEGS
F32 = jnp.float32
BF16 = jnp.bfloat16
MESH = pl.DeviceIdType.MESH


def kernel(t_ref, gain_ref, proj_ref, own_ref, seg_ref, ctx_ref, resid_ref, wout_ref,
           out_ref, loss_ref,
           tv, sc, pv, cv, rv, wv, part, zr2, zr1, xr, sq, scale, onehot, buckets, bw, arr, wts,
           hv, gv, gt, pg, rsv, lb, lt,
           ld_sem, pv_sem, core_s, core_r, wo_s, wo_r, wt_s, wt_r, sq_s, sq_r,
           z2_s, z2_r, z1_s, z1_r, xh_s, xh_r, ar_s, ar_r, rs_s, rs_r, l1_s, l1_r, l2_s, l2_r, my_sem):
    t = lax.axis_index("tp")
    f = lax.axis_index("fsdp")
    z, xh = t // 2, t % 2
    g, c = f // 2, f % 2

    def tp_dev(i):
        return (i, f)

    def fs_dev(i):
        return (t, i)

    def rcopy(src, dst, ss, rs, dev):
        return pltpu.make_async_remote_copy(src_ref=src, dst_ref=dst, send_sem=ss, recv_sem=rs,
                                            device_id=dev, device_id_type=MESH)

    z_up, z_dn = lax.rem(t + 2, TP), lax.rem(t + 6, TP)
    xh_peer = t + 1 - 2 * xh
    core_peer = f + 1 - 2 * c

    ld_t = pltpu.make_async_copy(t_ref, tv, ld_sem.at[0])
    ld_t.start()
    rels = (2, 1, 3, 0)

    def unit_copy(q, r, x):
        dest = lax.rem(z + rels[r], 4) * 2 + x
        col = pl.multiple_of(dest * COLS + q * HALF, HALF)
        u = (q * 4 + r) * 2 + x
        return pltpu.make_async_copy(proj_ref.at[:, pl.ds(col, HALF)], pv.at[u], pv_sem.at[u])

    for q in range(2):
        for r in range(4):
            for x in range(2):
                unit_copy(q, r, x).start()
    my_rows = pl.ds(pl.multiple_of(c * ROWS, ROWS), ROWS)
    ld_c = pltpu.make_async_copy(ctx_ref, cv.at[my_rows], ld_sem.at[1])
    ld_c.start()
    ld_r, ld_w = [], []
    for q in range(2):
        mine = pl.ds(pl.multiple_of(q * HALF + c * LANES, LANES), LANES)
        ld_r.append(pltpu.make_async_copy(resid_ref.at[:, mine], rv.at[q, my_rows], ld_sem.at[2 + q]))
        ld_w.append(pltpu.make_async_copy(
            wout_ref.at[:, mine], wv.at[pl.ds(pl.multiple_of(f * KB, KB), KB), pl.ds(q * LANES, LANES)],
            ld_sem.at[4 + q]))
    for cp in ld_r + ld_w:
        cp.start()

    barrier = pltpu.get_barrier_semaphore()

    def greet_fs(s, _):
        pl.semaphore_signal(barrier, inc=1, device_id=fs_dev(lax.rem(f + s, FS)), device_id_type=MESH)
        return 0

    def greet_tp(s, _):
        pl.semaphore_signal(barrier, inc=1, device_id=tp_dev(lax.rem(t + s, TP)), device_id_type=MESH)
        return 0

    lax.fori_loop(1, FS, greet_fs, 0)
    lax.fori_loop(1, TP, greet_tp, 0)

    own = own_ref[...]
    seg = seg_ref[...]
    marks = (lax.broadcasted_iota(jnp.int32, (FS, SLAB), 0) == own)
    earlier = (lax.broadcasted_iota(jnp.int32, (SLAB, SLAB), 0)
               < lax.broadcasted_iota(jnp.int32, (SLAB, SLAB), 1)).astype(F32).astype(BF16)
    marks = marks.astype(F32)
    before = jnp.dot(marks.astype(BF16), earlier, preferred_element_type=F32)
    rank = jnp.sum(before * marks, axis=0, keepdims=True).astype(jnp.int32)
    slot = own * CAP + rank
    onehot[...] = (lax.broadcasted_iota(jnp.int32, (ROWS, SLAB), 0) == slot).astype(F32).astype(BF16)
    member = (lax.broadcasted_iota(jnp.int32, (SEGS, SLAB), 0) == seg).astype(F32)
    counts = jnp.sum(member, axis=1, keepdims=True)
    length = jnp.sum(member * counts, axis=0, keepdims=True)
    weight = (1.0 / length).astype(BF16)
    bw[...] = lax.dot_general(onehot[...], jnp.broadcast_to(weight, (LANES, SLAB)), (((1,), (1,)), ((), ())),
                              preferred_element_type=F32).astype(BF16)

    ld_t.wait()

    def scale_step(i, _):
        rows = pl.ds(pl.multiple_of(i * 64, 64), 64)
        wide = tv[rows, :].astype(F32)
        sc[rows, :] = (wide * gain_ref[...]).astype(BF16)
        two = wide * wide
        acc = two[:, 0:LANES]
        for k in range(1, KT // LANES):
            acc = acc + two[:, k * LANES:(k + 1) * LANES]
        scale[rows, :] = acc
        return 0

    lax.fori_loop(0, SLAB // 64, scale_step, 0)
    sq[t] = jnp.broadcast_to(jnp.sum(scale[...].T, axis=0, keepdims=True), (8, SLAB))

    pl.semaphore_wait(barrier, FS - 1 + TP - 1)

    other = 1 - c
    cx = [rcopy(ctx_ref, cv.at[my_rows], core_s.at[0], core_r.at[0], fs_dev(core_peer))]
    for q in range(2):
        theirs = pl.ds(pl.multiple_of(q * HALF + other * LANES, LANES), LANES)
        cx.append(rcopy(resid_ref.at[:, theirs], rv.at[q, my_rows], core_s.at[1 + q], core_r.at[1 + q], fs_dev(core_peer)))

    def wo_copy(q, src, dst):
        lanes = pl.ds(pl.multiple_of(q * HALF + (dst % 2) * LANES, LANES), LANES)
        return rcopy(wout_ref.at[:, lanes],
                     wv.at[pl.ds(pl.multiple_of(src * KB, KB), KB), pl.ds(q * LANES, LANES)],
                     wo_s.at[q, dst], wo_r.at[q, src], fs_dev(dst))

    def wt_copy(src, dst):
        return rcopy(bw.at[pl.ds(pl.multiple_of((dst // 2) * 2 * CAP, 2 * CAP), 2 * CAP)], wts.at[src],
                     wt_s.at[dst], wt_r.at[src], fs_dev(dst))

    def sq_copy(src, dst):
        return rcopy(sq.at[src], sq.at[src], sq_s.at[dst], sq_r.at[src], tp_dev(dst))

    def each_fs(fn):
        def body(s, _):
            fn(lax.rem(f + s, FS))
            return 0
        lax.fori_loop(1, FS, body, 0)

    def each_tp(fn):
        def body(s, _):
            fn(lax.rem(t + s, TP))
            return 0
        lax.fori_loop(1, TP, body, 0)

    each_tp(lambda d: sq_copy(t, d).start())
    wt_mine = pltpu.make_async_copy(bw.at[pl.ds(pl.multiple_of(g * 2 * CAP, 2 * CAP), 2 * CAP)], wts.at[f], my_sem.at[0])
    wt_mine.start()

    def z2_copy(q, up):
        return rcopy(part.at[(q * 4 + 0) * 2 + up], zr2.at[q, up], z2_s.at[q, up], z2_r.at[q, up],
                     tp_dev(z_up if up else z_dn))

    def z1_copy(q, up, x):
        return rcopy(part.at[(q * 4 + (1 if up else 2)) * 2 + x], zr1.at[q, up, x],
                     z1_s.at[q, up, x], z1_r.at[q, up, x], tp_dev(z_up if up else z_dn))

    def product(q, r):
        for x in range(2):
            unit_copy(q, r, x).wait()

        def body(x, _):
            u = (q * 4 + r) * 2 + x
            part[u] = jnp.dot(sc[...], pv[u], preferred_element_type=F32).astype(BF16)
            return 0

        lax.fori_loop(0, 2, body, 0)

    def teacher_sends(q, r):
        if r == 0:
            z2_copy(q, 1).start()
            z2_copy(q, 0).start()
        elif r == 1:
            z1_copy(q, 1, 0).start()
        elif r == 2:
            z1_copy(q, 0, 1).start()

    def z_middle(q):
        for up in (1, 0):
            z2_copy(q, up).wait_recv()
            u = (q * 4 + (1 if up else 2)) * 2 + up
            part[u] = (part[u].astype(F32) + zr2[q, up].astype(F32)).astype(BF16)
            z1_copy(q, up, up).start()

    def z_last(q):
        for up in (1, 0):
            for x in range(2):
                z1_copy(q, up, x).wait_recv()

    def z_total(q, x):
        return (part[(q * 4 + 3) * 2 + x].astype(F32) + zr1[q, 0, x].astype(F32)) + zr1[q, 1, x].astype(F32)

    def xh_copy(q):
        return rcopy(part.at[(q * 4 + 3) * 2 + (1 - xh)], xr.at[q], xh_s.at[q], xh_r.at[q], tp_dev(xh_peer))

    def x_send(q):
        part[(q * 4 + 3) * 2 + (1 - xh)] = z_total(q, 1 - xh).astype(BF16)
        xh_copy(q).start()

    def ar_copy(q, src, dst):
        return rcopy(buckets.at[q, dst % 2, pl.ds(pl.multiple_of((dst // 2) * 2 * CAP, 2 * CAP), 2 * CAP)],
                     arr.at[q, src], ar_s.at[q, dst], ar_r.at[q, src], fs_dev(dst))

    def ar_mine(q):
        return pltpu.make_async_copy(
            buckets.at[q, c, pl.ds(pl.multiple_of(g * 2 * CAP, 2 * CAP), 2 * CAP)], arr.at[q, f], my_sem.at[1 + q])

    def regroup(q):
        xh_copy(q).wait_recv()
        raw = z_total(q, xh) + xr[q].astype(F32)
        by = scale[...]
        fitted = (raw * jnp.concatenate([by, by], axis=1)).astype(BF16)
        moved = jnp.dot(onehot[...], fitted, preferred_element_type=F32).astype(BF16)
        buckets[q, 0] = moved[:, :LANES]
        buckets[q, 1] = moved[:, LANES:]
        each_fs(lambda d: ar_copy(q, f, d).start())
        ar_mine(q).start()

    def rs_copy(q, src, dst):
        return rcopy(pg.at[q, dst], rsv.at[q, src], rs_s.at[q, dst], rs_r.at[q, src], fs_dev(dst))

    def rs_mine(q):
        return pltpu.make_async_copy(pg.at[q, f], rsv.at[q, f], my_sem.at[3 + q])

    def gradient(q, total):
        ar_mine(q).wait()

        def one(s, total):
            src = lax.rem(f + s, FS)

            @pl.when(s > 0)
            def _():
                ar_copy(q, src, f).wait_recv()

            for j in range(2):
                rows = pl.ds(pl.multiple_of(j * ROWS + src * CAP, CAP), CAP)
                diff = hv[rows, q * LANES:(q + 1) * LANES] - arr[q, src, j * CAP:(j + 1) * CAP, :].astype(F32)
                wd = wts[src, j * CAP:(j + 1) * CAP, :].astype(F32) * diff
                gv[rows, :] = wd * (2.0 / DENOM)
                terms = wd * diff
                for k in range(CAP // 8):
                    total = total + terms[k * 8:(k + 1) * 8]
            return total

        total = lax.fori_loop(0, FS, one, total)
        gt[...] = gv[...].T.astype(BF16)

        def term(i, _):
            dst = lax.rem(f + 1 + i, FS)
            cols = pl.ds(pl.multiple_of(dst * KB, KB), KB)
            pg[q, dst] = jnp.dot(gt[...], cv[:, cols], preferred_element_type=F32).astype(BF16)

            @pl.when(i < FS - 1)
            def _():
                rs_copy(q, f, dst).start()

            return 0

        lax.fori_loop(0, FS, term, 0)
        rs_mine(q).start()
        return total

    def collect(q):
        each_fs(lambda s: rs_copy(q, s, f).wait_recv())
        rs_mine(q).wait()
        for k in range(2):
            acc = rsv[q, k].astype(F32)
            for i in range(1, FS // 2):
                acc = acc + rsv[q, 2 * i + k].astype(F32)
            out_ref[q * HALF + k * LANES:q * HALF + (k + 1) * LANES, :] = acc.astype(BF16)

    for r in range(4):
        product(0, r)
        teacher_sends(0, r)
        if r == 0:
            for cp in cx:
                cp.start()
            each_fs(lambda d: wo_copy(0, f, d).start())
            each_fs(lambda d: wo_copy(1, f, d).start())
            each_fs(lambda d: wt_copy(f, d).start())
    z_middle(0)
    for r in range(4):
        product(1, r)
        teacher_sends(1, r)

    each_tp(lambda s: sq_copy(s, t).wait_recv())
    squares = sq[0]
    for i in range(1, TP):
        squares = squares + sq[i]
    rows_scale = lax.rsqrt(squares[0:1] / D_T + 1e-05)
    scale[...] = jnp.broadcast_to(rows_scale, (LANES, SLAB)).T

    z_middle(1)

    ld_c.wait()
    for cp in ld_r + ld_w:
        cp.wait()
    for cp in cx:
        cp.wait_recv()
    each_fs(lambda s: wo_copy(0, s, f).wait_recv())
    each_fs(lambda s: wo_copy(1, s, f).wait_recv())

    def hidden_step(i, _):
        rows = pl.ds(pl.multiple_of(i * 256, 256), 256)
        prod = jnp.dot(cv[rows, :], wv[...], preferred_element_type=F32)
        hv[rows, :] = prod + jnp.concatenate([rv[0, rows, :].astype(F32), rv[1, rows, :].astype(F32)], axis=1)
        return 0

    lax.fori_loop(0, 2 * ROWS // 256, hidden_step, 0)

    z_last(0)
    x_send(0)
    regroup(0)
    z_last(1)
    x_send(1)
    each_fs(lambda s: wt_copy(s, f).wait_recv())
    wt_mine.wait()
    total = gradient(0, jnp.zeros((8, LANES), F32))
    regroup(1)
    total = gradient(1, total)

    def l1_copy(src, dst):
        return rcopy(lb.at[src], lb.at[src], l1_s.at[dst], l1_r.at[src], fs_dev(dst))

    def l2_copy(src, dst):
        return rcopy(lt.at[src], lt.at[src], l2_s.at[dst], l2_r.at[src], tp_dev(dst))

    lb[f] = total
    each_fs(lambda d: l1_copy(f, d).start())
    collect(0)
    each_fs(lambda s: l1_copy(s, f).wait_recv())
    total = lb[0]
    for i in range(1, FS):
        total = total + lb[i]
    lt[t] = total
    each_tp(lambda d: l2_copy(t, d).start())
    collect(1)
    each_tp(lambda s: l2_copy(s, t).wait_recv())
    total = lt[0]
    for i in range(1, TP):
        total = total + lt[i]
    total = jnp.sum(jnp.sum(total, axis=0, keepdims=True), axis=1, keepdims=True) / DENOM
    loss_ref[...] = jnp.broadcast_to(total, (8, LANES))

    for cp in cx:
        cp.wait_send()
    for q in range(2):
        for up in range(2):
            z2_copy(q, up).wait_send()
            for x in range(2):
                z1_copy(q, up, x).wait_send()
        xh_copy(q).wait_send()

    def drain_fs(d):
        for q in range(2):
            wo_copy(q, f, d).wait_send()
            ar_copy(q, f, d).wait_send()
            rs_copy(q, f, d).wait_send()
        wt_copy(f, d).wait_send()
        l1_copy(f, d).wait_send()

    def drain_tp(d):
        sq_copy(t, d).wait_send()
        l2_copy(t, d).wait_send()

    each_fs(drain_fs)
    each_tp(drain_tp)


def per_device(t_hid, teacher_gain, proj, owner, seg_ids, student_ctx, student_resid, w_out):
    dma = pltpu.SemaphoreType.DMA
    anyspace = pl.BlockSpec(memory_space=pl.ANY)
    vmem = pl.BlockSpec(memory_space=pltpu.VMEM)
    out, loss = pl.pallas_call(
        kernel,
        out_shape=(jax.ShapeDtypeStruct((COLS, KB), BF16), jax.ShapeDtypeStruct((8, LANES), F32)),
        in_specs=[anyspace, vmem, anyspace, vmem, vmem, anyspace, anyspace, anyspace],
        out_specs=(vmem, vmem),
        scratch_shapes=[
            pltpu.VMEM((SLAB, KT), BF16),
            pltpu.VMEM((SLAB, KT), BF16),
            pltpu.VMEM((16, KT, HALF), BF16),
            pltpu.VMEM((2 * ROWS, D_S), BF16),
            pltpu.VMEM((2, 2 * ROWS, LANES), BF16),
            pltpu.VMEM((D_S, HALF), BF16),
            pltpu.VMEM((16, SLAB, HALF), BF16),
            pltpu.VMEM((2, 2, SLAB, HALF), BF16),
            pltpu.VMEM((2, 2, 2, SLAB, HALF), BF16),
            pltpu.VMEM((2, SLAB, HALF), BF16),
            pltpu.VMEM((TP, 8, SLAB), F32),
            pltpu.VMEM((SLAB, LANES), F32),
            pltpu.VMEM((ROWS, SLAB), BF16),
            pltpu.VMEM((2, 2, ROWS, LANES), BF16),
            pltpu.VMEM((ROWS, LANES), BF16),
            pltpu.VMEM((2, FS, 2 * CAP, LANES), BF16),
            pltpu.VMEM((FS, 2 * CAP, LANES), BF16),
            pltpu.VMEM((2 * ROWS, HALF), F32),
            pltpu.VMEM((2 * ROWS, LANES), F32),
            pltpu.VMEM((LANES, 2 * ROWS), BF16),
            pltpu.VMEM((2, FS, LANES, KB), BF16),
            pltpu.VMEM((2, FS, LANES, KB), BF16),
            pltpu.VMEM((FS, 8, LANES), F32),
            pltpu.VMEM((TP, 8, LANES), F32),
            dma((8,)), dma((16,)), dma((3,)), dma((3,)),
            dma((2, FS)), dma((2, FS)), dma((FS,)), dma((FS,)), dma((TP,)), dma((TP,)),
            dma((2, 2)), dma((2, 2)), dma((2, 2, 2)), dma((2, 2, 2)), dma((2,)), dma((2,)),
            dma((2, FS)), dma((2, FS)), dma((2, FS)), dma((2, FS)),
            dma((FS,)), dma((FS,)), dma((TP,)), dma((TP,)), dma((5,)),
        ],
        compiler_params=pltpu.CompilerParams(collective_id=0, has_side_effects=True, vmem_limit_bytes=62 << 20),
        cost_estimate=pl.CostEstimate(flops=15 * 10 ** 9, bytes_accessed=32 << 20, transcendentals=0),
    )(t_hid, teacher_gain.reshape(1, KT), proj, owner.reshape(1, SLAB), seg_ids, student_ctx, student_resid, w_out)
    return loss[0, 0], out.T


def solution(mesh):
    return jax.shard_map(
        per_device,
        mesh=mesh,
        in_specs=(
            P("fsdp", "tp"),
            P("tp"),
            P("tp", None),
            P("fsdp", None),
            P("fsdp", None),
            P("fsdp", None),
            P("fsdp", "tp"),
            P("fsdp", "tp"),
        ),
        out_specs=(P(), P("fsdp", "tp")),
        check_vma=False,
    )
```

```python
import jax
import jax.numpy as jnp
from jax import lax
from jax.experimental import pallas as pl
from jax.experimental.pallas import tpu as pltpu
from jax.sharding import PartitionSpec as P

D_T = 16384
D_S = 4096
SEGS = 8
TP = 8
FS = 16
SLAB = 512
KT = D_T // TP
COLS = D_S // TP
CAP = 48
ROWS = FS * CAP
KB = D_S // FS
HALF = COLS // 2
LANES = 128
DENOM = D_S * FS * SEGS
F32 = jnp.float32
BF16 = jnp.bfloat16
MESH = pl.DeviceIdType.MESH


def kernel(t_ref, gain_ref, proj_ref, own_ref, seg_ref, ctx_ref, resid_ref, wout_ref,
           out_ref, loss_ref,
           tv, sc, pv, cv, rv, wv, part, zr2, zr1, xr, sq, scale, onehot, buckets, bw, arr, wts, wcol,
           hv, gv, gt, pg, rsv, rsy, lb, lt,
           ld_sem, pv_sem, my_sem, core_s, core_r, w_s, wo_r, wy_r, wf_r, wg_r, wx_r, wt_s, wt_r, sq_s, sq_r,
           z_s, z2_r, z1_r, xh_r, ar_s, ar_r, rs_s, rs_r, ry_s, ry_r, l1_s, l1_r, l2_s, l2_r):
    t = lax.axis_index("tp")
    f = lax.axis_index("fsdp")
    z, xh = t // 2, t % 2
    g, c = f // 2, f % 2

    def tp_dev(i):
        return (i, f)

    def fs_dev(i):
        return (t, i)

    def rcopy(src, dst, ss, rs, dev):
        return pltpu.make_async_remote_copy(src_ref=src, dst_ref=dst, send_sem=ss, recv_sem=rs,
                                            device_id=dev, device_id_type=MESH)

    def arrived(view, sem):
        rcopy(view, view, sem, sem, fs_dev(core_peer)).wait_recv()

    def sent(view, sem):
        rcopy(view, view, sem, sem, fs_dev(core_peer)).wait_send()

    z_up, z_dn = lax.rem(t + 2, TP), lax.rem(t + 6, TP)
    xh_peer = t + 1 - 2 * xh
    core_peer = f + 1 - 2 * c
    y, xl = f // 4, g % 2
    xl_chip = g + 1 - 2 * xl

    barrier = pltpu.get_barrier_semaphore()

    def greet_fs(s, _):
        pl.semaphore_signal(barrier, inc=1, device_id=fs_dev(lax.rem(f + s, FS)), device_id_type=MESH)
        return 0

    def greet_tp(s, _):
        pl.semaphore_signal(barrier, inc=1, device_id=tp_dev(lax.rem(t + s, TP)), device_id_type=MESH)
        return 0

    lax.fori_loop(1, FS, greet_fs, 0)
    lax.fori_loop(1, TP, greet_tp, 0)

    ld_t = pltpu.make_async_copy(t_ref, tv, ld_sem.at[0])
    ld_t.start()
    rels = (2, 1, 3, 0)

    def unit_copy(q, r, x):
        dest = lax.rem(z + rels[r], 4) * 2 + x
        col = pl.multiple_of(dest * COLS + q * HALF, HALF)
        u = (q * 4 + r) * 2 + x
        return pltpu.make_async_copy(proj_ref.at[:, pl.ds(col, HALF)], pv.at[u], pv_sem.at[q * 4 + r])

    for x in range(2):
        unit_copy(0, 0, x).start()
    my_rows = pl.ds(pl.multiple_of(c * ROWS, ROWS), ROWS)
    ld_c = pltpu.make_async_copy(ctx_ref, cv.at[my_rows], ld_sem.at[1])
    ld_r, ld_w = [], []
    for q in range(2):
        mine = pl.ds(pl.multiple_of(q * HALF + c * LANES, LANES), LANES)
        ld_r.append(pltpu.make_async_copy(resid_ref.at[:, mine], rv.at[q, my_rows], ld_sem.at[2 + q]))
        ld_w.append(pltpu.make_async_copy(
            wout_ref.at[:, mine], wv.at[pl.ds(pl.multiple_of(f * KB, KB), KB), pl.ds(q * LANES, LANES)],
            ld_sem.at[4 + q]))
    own = own_ref[...]
    seg = seg_ref[...]
    marks = (lax.broadcasted_iota(jnp.int32, (FS, SLAB), 0) == own)
    earlier = (lax.broadcasted_iota(jnp.int32, (SLAB, SLAB), 0)
               < lax.broadcasted_iota(jnp.int32, (SLAB, SLAB), 1)).astype(F32).astype(BF16)
    marks = marks.astype(F32)
    before = jnp.dot(marks.astype(BF16), earlier, preferred_element_type=F32)
    rank = jnp.sum(before * marks, axis=0, keepdims=True).astype(jnp.int32)
    slot = own * CAP + rank
    onehot[...] = (lax.broadcasted_iota(jnp.int32, (ROWS, SLAB), 0) == slot).astype(F32).astype(BF16)
    member = (lax.broadcasted_iota(jnp.int32, (SEGS, SLAB), 0) == seg).astype(F32)
    counts = jnp.sum(member, axis=1, keepdims=True)
    length = jnp.sum(member * counts, axis=0, keepdims=True)
    weight = jnp.broadcast_to((1.0 / length).astype(BF16), (16, SLAB))
    wide_slot = (own // 2) * LANES + (own % 2) * CAP + rank
    spread = (lax.broadcasted_iota(jnp.int32, (FS // 2 * LANES, SLAB), 0) == wide_slot).astype(F32).astype(BF16)
    moved = lax.dot_general(weight, spread, (((1,), (1,)), ((), ())), preferred_element_type=F32)
    for i in range(FS // 2):
        bw[i] = moved[0:8, i * LANES:(i + 1) * LANES]

    ld_t.wait()
    for q in range(2):
        for r in range(4):
            for x in range(2):
                if q or r:
                    unit_copy(q, r, x).start()
    for cp in ld_w + ld_r + [ld_c]:
        cp.start()

    def scale_step(i, _):
        rows = pl.ds(pl.multiple_of(i * 64, 64), 64)
        wide = tv[rows, :].astype(F32)
        sc[rows, :] = (wide * gain_ref[...]).astype(BF16)
        two = wide * wide
        acc = two[:, 0:LANES]
        for k in range(1, KT // LANES):
            acc = acc + two[:, k * LANES:(k + 1) * LANES]
        scale[rows, :] = acc
        return 0

    lax.fori_loop(0, SLAB // 64, scale_step, 0)
    row = jnp.sum(scale[...].T, axis=0, keepdims=True)
    sq[t] = jnp.concatenate([row[:, i * LANES:(i + 1) * LANES] for i in range(4)] * 2, axis=0)

    other = 1 - c
    cx = [rcopy(ctx_ref, cv.at[my_rows], core_s, core_r, fs_dev(core_peer))]
    for q in range(2):
        theirs = pl.ds(pl.multiple_of(q * HALF + other * LANES, LANES), LANES)
        cx.append(rcopy(resid_ref.at[:, theirs], rv.at[q, my_rows], core_s, core_r, fs_dev(core_peer)))

    def wo_copy(q, src, dst, lane):
        lanes = pl.ds(pl.multiple_of(q * HALF + (dst % 2) * LANES, LANES), LANES)
        return rcopy(wout_ref.at[:, lanes],
                     wv.at[pl.ds(pl.multiple_of(src * KB, KB), KB), pl.ds(q * LANES, LANES)],
                     w_s, wo_r.at[lane], fs_dev(dst))

    def wt_copy(src, dst):
        return rcopy(bw.at[dst // 2], wts.at[src],
                     wt_s, wt_r, fs_dev(dst))

    def sq_copy(src, dst):
        return rcopy(sq.at[src], sq.at[src], sq_s, sq_r, tp_dev(dst))

    def each_fs(fn):
        def body(s, _):
            fn(lax.rem(f + s, FS))
            return 0
        lax.fori_loop(1, FS, body, 0)

    def each_tp(fn):
        def body(s, _):
            fn(lax.rem(t + s, TP))
            return 0
        lax.fori_loop(1, TP, body, 0)

    wt_mine = pltpu.make_async_copy(bw.at[g], wts.at[f], my_sem.at[0])
    wt_mine.start()

    near_chips = (core_peer, 2 * xl_chip, 2 * xl_chip + 1)

    def w_rows(yy):
        return pl.ds(pl.multiple_of(yy * 4 * KB, 4 * KB), 4 * KB)

    y_up, y_dn, y_far = lax.rem(y + 1, 4), lax.rem(y + 3, 4), lax.rem(y + 2, 4)

    def y_dev(yy):
        return fs_dev(yy * 4 + xl * 2 + c)

    def y_side(up):
        return y_dev(y_up if up else y_dn)

    def wy_copy(up, rows):
        view = wv.at[rows, 0:LANES]
        return rcopy(view, view, w_s, wy_r.at[up], y_side(up))

    def wf_copy(up, yy):
        view = wv.at[pl.ds(pl.multiple_of(yy * 4 * KB + (0 if up else 2 * KB), 2 * KB), 2 * KB), 0:LANES]
        return rcopy(view, view, w_s, wf_r, y_side(up))

    def wg_copy(up, yy):
        src = yy * 4 + xl * 2 + (0 if up else 1)
        view = wv.at[pl.ds(pl.multiple_of(src * KB, KB), KB), LANES:HALF]
        return rcopy(view, view, w_s, wg_r, y_side(up))

    def wx_copy(yy, side):
        view = wv.at[pl.ds(pl.multiple_of((yy * 2 + side) * 2 * KB, 2 * KB), 2 * KB), LANES:HALF]
        return rcopy(view, view, w_s, wx_r.at[yy], fs_dev(2 * xl_chip + c))

    def y_cores(yy):
        return (yy * 4 + xl * 2, yy * 4 + xl * 2 + 1)

    def wo_stage(n):
        if n == 0:
            wo_copy(1, f, core_peer, 0).start()
            for d in y_cores(y_up):
                wo_copy(1, f, d, 1).start()
            for d in y_cores(y_dn):
                wo_copy(1, f, d, 2).start()
            for d in near_chips:
                wo_copy(0, f, d, 3).start()
        elif n == 1:
            ld_w[1].wait()
            wo_copy(1, core_peer, f, 0).wait_recv()
            wx_copy(y, xl).start()
        elif n == 2:
            ld_w[0].wait()
            arrived(wv.at[0:3 * KB, 0:LANES], wo_r.at[3])
            wy_copy(1, w_rows(y)).start()
            wy_copy(0, w_rows(y)).start()
            for up, yy in ((1, y_dn), (0, y_up)):
                arrived(wv.at[0:2 * KB, LANES:HALF], wo_r.at[2 - up])
                wg_copy(up, yy).start()
                wx_copy(yy, xl).start()
        elif n == 3:
            arrived(wv.at[0:2 * KB, LANES:HALF], wg_r)
            wx_copy(y_far, xl).start()
        else:
            wy_copy(1, w_rows(y_dn)).wait_recv()
            wf_copy(1, y_dn).start()
            wy_copy(0, w_rows(y_up)).wait_recv()
            wf_copy(0, y_up).start()

    def hidden(n):
        yy = (y, y_dn, y_up, y_far)[n]
        if n == 0:
            ld_c.wait()
            for cp in ld_r:
                cp.wait()
            arrived(cv.at[0:ROWS + ROWS * HALF // D_S], core_r)
        if n == 3:
            arrived(wv.at[0:4 * KB, 0:LANES], wf_r)
        wx_copy(yy, 1 - xl).wait_recv()

        def step(i, _):
            rows = pl.ds(pl.multiple_of(i * 512, 512), 512)
            depth = pl.ds(pl.multiple_of(yy * 4 * KB, 4 * KB), 4 * KB)
            prod = jnp.dot(cv[rows, depth], wv[w_rows(yy), :], preferred_element_type=F32)
            if n == 0:
                before = jnp.concatenate([rv[0, rows, :].astype(F32), rv[1, rows, :].astype(F32)], axis=1)
            else:
                before = hv[rows, :]
            hv[rows, :] = prod + before
            return 0

        lax.fori_loop(0, 2 * ROWS // 512, step, 0)

    def columns_of_weights():
        arrived(wts.at[0:FS - 1], wt_r)
        wt_mine.wait()

        def one(i, _):
            wcol[i] = jnp.broadcast_to(wts[i][0:1], (LANES, LANES)).T
            return 0

        lax.fori_loop(0, FS, one, 0)

    def piece(k, r, x):
        return (k * 4 + r) * 2 + x

    def z2_copy(k, up):
        return rcopy(part.at[piece(k, 0, up)], zr2.at[k, up], z_s, z2_r.at[k, up],
                     tp_dev(z_up if up else z_dn))

    def z1_copy(k, up, x):
        return rcopy(part.at[piece(k, 1 if up else 2, x)], zr1.at[k, up, x],
                     z_s, z1_r.at[k], tp_dev(z_up if up else z_dn))

    def product(q, r):
        first = (q * 4 + r) * 2
        pltpu.make_async_copy(pv.at[pl.ds(first, 2)], pv.at[pl.ds(first, 2)], pv_sem.at[q * 4 + r]).wait()

        def body(x, _):
            both = jnp.dot(sc[...], pv[(q * 4 + r) * 2 + x], preferred_element_type=F32).astype(BF16)
            part[piece(2 * q, r, x)] = both[:, :LANES]
            part[piece(2 * q + 1, r, x)] = both[:, LANES:]
            return 0

        lax.fori_loop(0, 2, body, 0)

    def z_far(k):
        z2_copy(k, 1).start()
        z2_copy(k, 0).start()

    def z_near(k, up):
        z1_copy(k, up, 1 - up).start()

    def z_middle(k):
        for up in (1, 0):
            z2_copy(k, up).wait_recv()
            u = piece(k, 1 if up else 2, up)
            part[u] = (part[u].astype(F32) + zr2[k, up].astype(F32)).astype(BF16)
            z1_copy(k, up, up).start()

    def z_total(k, x):
        return (part[piece(k, 3, x)].astype(F32) + zr1[k, 0, x].astype(F32)) + zr1[k, 1, x].astype(F32)

    def xh_copy(k):
        return rcopy(part.at[piece(k, 3, 1 - xh)], xr.at[k], z_s, xh_r.at[k], tp_dev(xh_peer))

    def z_last(k):
        arrived(zr1.at[k], z1_r.at[k])
        part[piece(k, 3, 1 - xh)] = z_total(k, 1 - xh).astype(BF16)
        xh_copy(k).start()

    def ar_copy(k, src, dst):
        return rcopy(buckets.at[k, pl.ds(pl.multiple_of((dst // 2) * 2 * CAP, 2 * CAP), 2 * CAP)],
                     arr.at[k // 2, src], ar_s, ar_r.at[k // 2], fs_dev(dst))

    def ar_mine(k):
        return pltpu.make_async_copy(
            buckets.at[k, pl.ds(pl.multiple_of(g * 2 * CAP, 2 * CAP), 2 * CAP)], arr.at[k // 2, f], my_sem.at[1 + k // 2])

    def each_owner(k, fn):
        def body(s, _):
            fn(2 * lax.rem(g + s, FS // 2) + k % 2)
            return 0

        lax.fori_loop(1, FS // 2, body, 0)

        @pl.when(c != k % 2)
        def _():
            fn(core_peer)

    def regroup(k):
        xh_copy(k).wait_recv()
        raw = z_total(k, xh) + xr[k].astype(F32)
        fitted = (raw * scale[...]).astype(BF16)
        buckets[k] = jnp.dot(onehot[...], fitted, preferred_element_type=F32).astype(BF16)
        each_owner(k, lambda d: ar_copy(k, f, d).start())

        @pl.when(c == k % 2)
        def _():
            ar_mine(k).start()

    def rs_copy(q, src, dst):
        return rcopy(pg.at[q, dst], rsv.at[q, src], rs_s, rs_r.at[2 * q + src % 2], fs_dev(dst))

    def rs_mine(q):
        return pltpu.make_async_copy(pg.at[q, f], rsv.at[q, f], my_sem.at[3 + q])

    def ry_copy(src, dst):
        return rcopy(pg.at[0, pl.ds(dst * 4, 4)], rsy.at[src], ry_s, ry_r, y_dev(dst))

    def rs_mid(k):
        @pl.when(c == k % 2)
        def _():
            arrived(rsy.at[0:3], ry_r)
            for i in range(4):
                acc = pg[0, y * 4 + i].astype(F32)
                for s in range(1, 4):
                    acc = acc + rsy[lax.rem(y + s, 4), i].astype(F32)
                pg[0, y * 4 + i] = acc.astype(BF16)
            for d in near_chips:
                rs_copy(0, f, d).start()
            rs_mine(0).start()

    def gradient(q):
        def one(s, total):
            src = lax.rem(f + s, FS)

            for j in range(2):
                rows = pl.ds(pl.multiple_of(j * ROWS + src * CAP, CAP), CAP)
                diff = hv[rows, q * LANES:(q + 1) * LANES] - arr[q, src, j * CAP:(j + 1) * CAP, :].astype(F32)
                wd = wcol[src, j * CAP:(j + 1) * CAP, :] * diff
                gv[rows, :] = wd * (2.0 / DENOM)
                terms = wd * diff
                for k in range(CAP // 8):
                    total = total + terms[k * 8:(k + 1) * 8]
            return total

        total = lb[f] if q else jnp.zeros((8, LANES), F32)
        lb[f] = lax.fori_loop(0, FS, one, total)
        if q:
            each_fs(lambda d: l1_copy(f, d).start())
        gt[...] = gv[...].T.astype(BF16)

        def term(i, _):
            dst = lax.rem((y + 2) * 4 + i, FS) if q == 0 else lax.rem(f + 1 + i, FS)
            cols = pl.ds(pl.multiple_of(dst * KB, KB), KB)
            pg[q, dst] = jnp.dot(gt[...], cv[:, cols], preferred_element_type=F32).astype(BF16)
            if q:
                @pl.when(i < FS - 1)
                def _():
                    rs_copy(q, f, dst).start()
            else:
                @pl.when((i % 4 == 3) & (dst // 4 != y))
                def _():
                    ry_copy(y, dst // 4).start()

            return 0

        if q:
            lax.fori_loop(0, FS, term, 0)
            rs_mine(q).start()
        else:
            for n in (0, 3, 1, 2):
                lax.fori_loop(4 * n, 4 * n + 4, term, 0)

    def student(k):
        @pl.when(c == k % 2)
        def _():
            ar_mine(k).wait()
            arrived(arr.at[k // 2, 0:FS - 1], ar_r.at[k // 2])
            gradient(k // 2)

    def collect(k):
        q, h = k // 2, k % 2

        count = FS // 2 if q else 2

        @pl.when(c == h)
        def _():
            rs_mine(q).wait()
            arrived(rsv.at[q, 0:count - 1], rs_r.at[k])

        @pl.when(c != h)
        def _():
            arrived(rsv.at[q, 0:count], rs_r.at[k])

        if q:
            acc = rsv[q, h].astype(F32)
            for i in range(1, FS // 2):
                acc = acc + rsv[q, 2 * i + h].astype(F32)
        else:
            acc = rsv[q, 2 * g + h].astype(F32) + rsv[q, 2 * xl_chip + h].astype(F32)
        out_ref[q * HALF + h * LANES:q * HALF + (h + 1) * LANES, :] = acc.astype(BF16)

    def l1_copy(src, dst):
        return rcopy(lb.at[src], lb.at[src], l1_s, l1_r, fs_dev(dst))

    def l2_copy(src, dst):
        return rcopy(lt.at[src], lt.at[src], l2_s, l2_r, tp_dev(dst))

    def row_scales():
        arrived(sq.at[0:TP - 1], sq_r)
        squares = sq[0]
        for i in range(1, TP):
            squares = squares + sq[i]
        rows_scale = lax.rsqrt(squares / D_T + 1e-05)
        for i in range(4):
            scale[i * LANES:(i + 1) * LANES, :] = jnp.broadcast_to(rows_scale[i:i + 1], (LANES, LANES)).T

    def loss_a():
        arrived(lb.at[0:FS - 1], l1_r)
        total = lb[0]
        for i in range(1, FS):
            total = total + lb[i]
        lt[t] = total
        each_tp(lambda d: l2_copy(t, d).start())

    def loss_b():
        arrived(lt.at[0:TP - 1], l2_r)
        total = lt[0]
        for i in range(1, TP):
            total = total + lt[i]
        total = jnp.sum(jnp.sum(total, axis=0, keepdims=True), axis=1, keepdims=True) / DENOM
        loss_ref[...] = jnp.broadcast_to(total, (8, LANES))

    product(0, 0)
    pl.semaphore_wait(barrier, FS - 1 + TP - 1)
    z_far(0)
    wo_stage(0)
    for cp in cx:
        cp.start()
    each_tp(lambda d: sq_copy(t, d).start())
    product(0, 1)
    z_near(0, 1)
    wo_stage(1)
    product(0, 2)
    z_near(0, 0)
    z_far(1)
    each_fs(lambda d: wt_copy(f, d).start())
    product(0, 3)
    z_middle(0)
    z_near(1, 1)
    z_near(1, 0)
    wo_stage(2)
    product(1, 0)
    z_far(2)
    product(1, 1)
    product(1, 2)
    z_middle(1)
    z_near(2, 1)
    z_near(2, 0)
    z_far(3)
    product(1, 3)
    row_scales()
    z_last(0)
    wo_stage(3)
    wo_stage(4)
    hidden(0)
    columns_of_weights()
    z_middle(2)
    z_near(3, 1)
    z_near(3, 0)
    regroup(0)
    z_last(1)
    hidden(1)
    hidden(2)
    z_middle(3)
    regroup(1)
    hidden(3)
    z_last(2)
    student(0)
    student(1)
    regroup(2)
    z_last(3)
    regroup(3)
    student(2)
    student(3)
    rs_mid(0)
    rs_mid(1)
    loss_a()
    collect(0)
    collect(1)
    collect(2)
    collect(3)
    loss_b()

    sent(cv.at[0:ROWS + ROWS * HALF // D_S], core_s)
    sent(wv.at[0:15 * KB], w_s)
    sent(part.at[0:28], z_s)
    sent(arr.at[:, 0:FS - 1], ar_s)
    sent(rsv.at[:, 0:9], rs_s)
    sent(pg.at[0, 0:12], ry_s)
    sent(wts.at[0:FS - 1], wt_s)
    sent(lb.at[0:FS - 1], l1_s)
    sent(lt.at[0:TP - 1], l2_s)
    sent(sq.at[0:TP - 1], sq_s)


def per_device(t_hid, teacher_gain, proj, owner, seg_ids, student_ctx, student_resid, w_out):
    dma = pltpu.SemaphoreType.DMA
    anyspace = pl.BlockSpec(memory_space=pl.ANY)
    vmem = pl.BlockSpec(memory_space=pltpu.VMEM)
    out, loss = pl.pallas_call(
        kernel,
        out_shape=(jax.ShapeDtypeStruct((COLS, KB), BF16), jax.ShapeDtypeStruct((8, LANES), F32)),
        in_specs=[anyspace, vmem, anyspace, vmem, vmem, anyspace, anyspace, anyspace],
        out_specs=(vmem, vmem),
        scratch_shapes=[
            pltpu.VMEM((SLAB, KT), BF16),
            pltpu.VMEM((SLAB, KT), BF16),
            pltpu.VMEM((16, KT, HALF), BF16),
            pltpu.VMEM((2 * ROWS, D_S), BF16),
            pltpu.VMEM((2, 2 * ROWS, LANES), BF16),
            pltpu.VMEM((D_S, HALF), BF16),
            pltpu.VMEM((32, SLAB, LANES), BF16),
            pltpu.VMEM((4, 2, SLAB, LANES), BF16),
            pltpu.VMEM((4, 2, 2, SLAB, LANES), BF16),
            pltpu.VMEM((4, SLAB, LANES), BF16),
            pltpu.VMEM((TP, 8, LANES), F32),
            pltpu.VMEM((SLAB, LANES), F32),
            pltpu.VMEM((ROWS, SLAB), BF16),
            pltpu.VMEM((4, ROWS, LANES), BF16),
            pltpu.VMEM((FS // 2, 8, LANES), F32),
            pltpu.VMEM((2, FS, 2 * CAP, LANES), BF16),
            pltpu.VMEM((FS, 8, LANES), F32),
            pltpu.VMEM((FS, LANES, LANES), F32),
            pltpu.VMEM((2 * ROWS, HALF), F32),
            pltpu.VMEM((2 * ROWS, LANES), F32),
            pltpu.VMEM((LANES, 2 * ROWS), BF16),
            pltpu.VMEM((2, FS, LANES, KB), BF16),
            pltpu.VMEM((2, FS, LANES, KB), BF16),
            pltpu.VMEM((4, 4, LANES, KB), BF16),
            pltpu.VMEM((FS, 8, LANES), F32),
            pltpu.VMEM((TP, 8, LANES), F32),
            dma((6,)), dma((8,)), dma((5,)), dma, dma, dma, dma((4,)), dma((2,)), dma, dma, dma((4,)),
            dma, dma, dma, dma, dma, dma((4, 2)), dma((4,)), dma((4,)), dma, dma((2,)), dma, dma((4,)),
            dma, dma, dma, dma, dma, dma,
        ],
        compiler_params=pltpu.CompilerParams(collective_id=0, has_side_effects=True, vmem_limit_bytes=62 << 20),
        cost_estimate=pl.CostEstimate(flops=15 * 10 ** 9, bytes_accessed=32 << 20, transcendentals=0),
    )(t_hid, teacher_gain.reshape(1, KT), proj, owner.reshape(1, SLAB), seg_ids, student_ctx, student_resid, w_out)
    return loss[0, 0], out.T


def solution(mesh):
    return jax.shard_map(
        per_device,
        mesh=mesh,
        in_specs=(
            P("fsdp", "tp"),
            P("tp"),
            P("tp", None),
            P("fsdp", None),
            P("fsdp", None),
            P("fsdp", None),
            P("fsdp", "tp"),
            P("fsdp", "tp"),
        ),
        out_specs=(P(), P("fsdp", "tp")),
        check_vma=False,
    )
```

```python
import jax
import jax.numpy as jnp
from jax import lax
from jax.experimental import pallas as pl
from jax.experimental.pallas import tpu as pltpu
from jax.sharding import PartitionSpec as P

D_T = 16384
D_S = 4096
SEGS = 8
TP = 8
FS = 16
SLAB = 512
KT = D_T // TP
COLS = D_S // TP
CAP = 48
ROWS = FS * CAP
KB = D_S // FS
HALF = COLS // 2
LANES = 128
DENOM = D_S * FS * SEGS
F32 = jnp.float32
BF16 = jnp.bfloat16
MESH = pl.DeviceIdType.MESH


def kernel(t_ref, gain_ref, proj_ref, own_ref, seg_ref, ctx_ref, resid_ref, wout_ref,
           out_ref, loss_ref,
           tv, sc, pv, cv, rv, wv, part, zr2, zr1, xr, sq, scale, onehot, buckets, bw, arr, wts, wcol,
           hv, gv, gt, pg, rsv, rsf, rsy, lb, lt,
           ld_sem, pv_sem, my_sem, core_s, core_r, w_s, wo_r, wy_r, wf_r, wg_r, wx_r, wt_s, wt_r, sq_s, sq_r,
           z_s, z2_r, z1_r, xh_r, ar_s, ar_r, rs_s, rs_r, rf_r, ry_s, ry_r, l1_s, l1_r, l2_s, l2_r):
    t = lax.axis_index("tp")
    f = lax.axis_index("fsdp")
    z, xh = t // 2, t % 2
    g, c = f // 2, f % 2

    def tp_dev(i):
        return (i, f)

    def fs_dev(i):
        return (t, i)

    def rcopy(src, dst, ss, rs, dev):
        return pltpu.make_async_remote_copy(src_ref=src, dst_ref=dst, send_sem=ss, recv_sem=rs,
                                            device_id=dev, device_id_type=MESH)

    def arrived(view, sem):
        rcopy(view, view, sem, sem, fs_dev(core_peer)).wait_recv()

    def sent(view, sem):
        rcopy(view, view, sem, sem, fs_dev(core_peer)).wait_send()

    z_up, z_dn = lax.rem(t + 2, TP), lax.rem(t + 6, TP)
    xh_peer = t + 1 - 2 * xh
    core_peer = f + 1 - 2 * c
    y, xl = f // 4, g % 2
    xl_chip = g + 1 - 2 * xl

    barrier = pltpu.get_barrier_semaphore()

    def greet_fs(s, _):
        pl.semaphore_signal(barrier, inc=1, device_id=fs_dev(lax.rem(f + s, FS)), device_id_type=MESH)
        return 0

    def greet_tp(s, _):
        pl.semaphore_signal(barrier, inc=1, device_id=tp_dev(lax.rem(t + s, TP)), device_id_type=MESH)
        return 0

    lax.fori_loop(1, FS, greet_fs, 0)
    lax.fori_loop(1, TP, greet_tp, 0)

    ld_t = pltpu.make_async_copy(t_ref, tv, ld_sem.at[0])
    ld_t.start()
    rels = (2, 1, 3, 0)

    def unit_copy(q, r, x):
        dest = lax.rem(z + rels[r], 4) * 2 + x
        col = pl.multiple_of(dest * COLS + q * HALF, HALF)
        u = (q * 4 + r) * 2 + x
        return pltpu.make_async_copy(proj_ref.at[:, pl.ds(col, HALF)], pv.at[u], pv_sem.at[q * 4 + r])

    for x in range(2):
        unit_copy(0, 0, x).start()
    my_rows = pl.ds(pl.multiple_of(c * ROWS, ROWS), ROWS)
    ld_c = pltpu.make_async_copy(ctx_ref, cv.at[my_rows], ld_sem.at[1])
    ld_r, ld_w = [], []
    for q in range(2):
        mine = pl.ds(pl.multiple_of(q * HALF + c * LANES, LANES), LANES)
        ld_r.append(pltpu.make_async_copy(resid_ref.at[:, mine], rv.at[q, my_rows], ld_sem.at[2 + q]))
        ld_w.append(pltpu.make_async_copy(
            wout_ref.at[:, mine], wv.at[pl.ds(pl.multiple_of(f * KB, KB), KB), pl.ds(q * LANES, LANES)],
            ld_sem.at[4 + q]))
    own = own_ref[...]
    seg = seg_ref[...]
    marks = (lax.broadcasted_iota(jnp.int32, (FS, SLAB), 0) == own)
    earlier = (lax.broadcasted_iota(jnp.int32, (SLAB, SLAB), 0)
               < lax.broadcasted_iota(jnp.int32, (SLAB, SLAB), 1)).astype(F32).astype(BF16)
    marks = marks.astype(F32)
    before = jnp.dot(marks.astype(BF16), earlier, preferred_element_type=F32)
    rank = jnp.sum(before * marks, axis=0, keepdims=True).astype(jnp.int32)
    slot = own * CAP + rank
    onehot[...] = (lax.broadcasted_iota(jnp.int32, (ROWS, SLAB), 0) == slot).astype(F32).astype(BF16)
    member = (lax.broadcasted_iota(jnp.int32, (SEGS, SLAB), 0) == seg).astype(F32)
    counts = jnp.sum(member, axis=1, keepdims=True)
    length = jnp.sum(member * counts, axis=0, keepdims=True)
    weight = jnp.broadcast_to((1.0 / length).astype(BF16), (16, SLAB))
    wide_slot = (own // 2) * LANES + (own % 2) * CAP + rank
    spread = (lax.broadcasted_iota(jnp.int32, (FS // 2 * LANES, SLAB), 0) == wide_slot).astype(F32).astype(BF16)
    moved = lax.dot_general(weight, spread, (((1,), (1,)), ((), ())), preferred_element_type=F32)
    for i in range(FS // 2):
        bw[i] = moved[0:8, i * LANES:(i + 1) * LANES]

    ld_t.wait()
    for q in range(2):
        for r in range(4):
            for x in range(2):
                if q or r:
                    unit_copy(q, r, x).start()
    for cp in ld_w + ld_r + [ld_c]:
        cp.start()

    def scale_step(i, _):
        rows = pl.ds(pl.multiple_of(i * 64, 64), 64)
        wide = tv[rows, :].astype(F32)
        sc[rows, :] = (wide * gain_ref[...]).astype(BF16)
        two = wide * wide
        acc = two[:, 0:LANES]
        for k in range(1, KT // LANES):
            acc = acc + two[:, k * LANES:(k + 1) * LANES]
        scale[rows, :] = acc
        return 0

    lax.fori_loop(0, SLAB // 64, scale_step, 0)
    row = jnp.sum(scale[...].T, axis=0, keepdims=True)
    sq[t] = jnp.concatenate([row[:, i * LANES:(i + 1) * LANES] for i in range(4)] * 2, axis=0)

    other = 1 - c
    cx = [rcopy(ctx_ref, cv.at[my_rows], core_s, core_r, fs_dev(core_peer))]
    for q in range(2):
        theirs = pl.ds(pl.multiple_of(q * HALF + other * LANES, LANES), LANES)
        cx.append(rcopy(resid_ref.at[:, theirs], rv.at[q, my_rows], core_s, core_r, fs_dev(core_peer)))

    def wo_copy(q, src, dst, lane):
        lanes = pl.ds(pl.multiple_of(q * HALF + (dst % 2) * LANES, LANES), LANES)
        return rcopy(wout_ref.at[:, lanes],
                     wv.at[pl.ds(pl.multiple_of(src * KB, KB), KB), pl.ds(q * LANES, LANES)],
                     w_s, wo_r.at[lane], fs_dev(dst))

    def wt_copy(src, dst):
        return rcopy(bw.at[dst // 2], wts.at[src],
                     wt_s, wt_r, fs_dev(dst))

    def sq_copy(src, dst):
        return rcopy(sq.at[src], sq.at[src], sq_s, sq_r, tp_dev(dst))

    def each_fs(fn):
        def body(s, _):
            fn(lax.rem(f + s, FS))
            return 0
        lax.fori_loop(1, FS, body, 0)

    def each_tp(fn):
        def body(s, _):
            fn(lax.rem(t + s, TP))
            return 0
        lax.fori_loop(1, TP, body, 0)

    wt_mine = pltpu.make_async_copy(bw.at[g], wts.at[f], my_sem.at[0])
    wt_mine.start()

    near_chips = (core_peer, 2 * xl_chip, 2 * xl_chip + 1)

    def w_rows(yy):
        return pl.ds(pl.multiple_of(yy * 4 * KB, 4 * KB), 4 * KB)

    y_up, y_dn, y_far = lax.rem(y + 1, 4), lax.rem(y + 3, 4), lax.rem(y + 2, 4)

    def y_dev(yy):
        return fs_dev(yy * 4 + xl * 2 + c)

    def y_side(up):
        return y_dev(y_up if up else y_dn)

    def wy_copy(up, rows):
        view = wv.at[rows, 0:LANES]
        return rcopy(view, view, w_s, wy_r.at[up], y_side(up))

    def wf_copy(up, yy):
        view = wv.at[pl.ds(pl.multiple_of(yy * 4 * KB + (0 if up else 2 * KB), 2 * KB), 2 * KB), 0:LANES]
        return rcopy(view, view, w_s, wf_r, y_side(up))

    def wg_copy(up, yy):
        src = yy * 4 + xl * 2 + (0 if up else 1)
        view = wv.at[pl.ds(pl.multiple_of(src * KB, KB), KB), LANES:HALF]
        return rcopy(view, view, w_s, wg_r, y_side(up))

    def wx_copy(yy, side):
        view = wv.at[pl.ds(pl.multiple_of((yy * 2 + side) * 2 * KB, 2 * KB), 2 * KB), LANES:HALF]
        return rcopy(view, view, w_s, wx_r.at[yy], fs_dev(2 * xl_chip + c))

    def y_cores(yy):
        return (yy * 4 + xl * 2, yy * 4 + xl * 2 + 1)

    def wo_stage(n):
        if n == 0:
            wo_copy(1, f, core_peer, 0).start()
            for d in y_cores(y_up):
                wo_copy(1, f, d, 1).start()
            for d in y_cores(y_dn):
                wo_copy(1, f, d, 2).start()
            for d in near_chips:
                wo_copy(0, f, d, 3).start()
        elif n == 1:
            ld_w[1].wait()
            wo_copy(1, core_peer, f, 0).wait_recv()
            wx_copy(y, xl).start()
        elif n == 2:
            for up, yy in ((1, y_dn), (0, y_up)):
                arrived(wv.at[0:2 * KB, LANES:HALF], wo_r.at[2 - up])
                wg_copy(up, yy).start()
                wx_copy(yy, xl).start()
            ld_w[0].wait()
            arrived(wv.at[0:3 * KB, 0:LANES], wo_r.at[3])
            wy_copy(1, w_rows(y)).start()
            wy_copy(0, w_rows(y)).start()
        elif n == 3:
            arrived(wv.at[0:2 * KB, LANES:HALF], wg_r)
            wx_copy(y_far, xl).start()
        else:
            wy_copy(1, w_rows(y_dn)).wait_recv()
            wf_copy(1, y_dn).start()
            wy_copy(0, w_rows(y_up)).wait_recv()
            wf_copy(0, y_up).start()

    def hidden(n):
        yy = (y, y_dn, y_up, y_far)[n]
        if n == 0:
            ld_c.wait()
            for cp in ld_r:
                cp.wait()
            arrived(cv.at[0:ROWS + ROWS * HALF // D_S], core_r)
        if n == 3:
            arrived(wv.at[0:4 * KB, 0:LANES], wf_r)
        wx_copy(yy, 1 - xl).wait_recv()

        def step(i, _):
            rows = pl.ds(pl.multiple_of(i * 512, 512), 512)
            depth = pl.ds(pl.multiple_of(yy * 4 * KB, 4 * KB), 4 * KB)
            prod = jnp.dot(cv[rows, depth], wv[w_rows(yy), :], preferred_element_type=F32)
            if n == 0:
                before = jnp.concatenate([rv[0, rows, :].astype(F32), rv[1, rows, :].astype(F32)], axis=1)
            else:
                before = hv[rows, :]
            hv[rows, :] = prod + before
            return 0

        lax.fori_loop(0, 2 * ROWS // 512, step, 0)

    def columns_of_weights():
        arrived(wts.at[0:FS - 1], wt_r)
        wt_mine.wait()

        def one(i, _):
            wcol[i] = jnp.broadcast_to(wts[i][0:1], (LANES, LANES)).T
            return 0

        lax.fori_loop(0, FS, one, 0)

    def piece(k, r, x):
        return (k * 4 + r) * 2 + x

    def z2_copy(k, up):
        return rcopy(part.at[piece(k, 0, up)], zr2.at[k, up], z_s, z2_r.at[k, up],
                     tp_dev(z_up if up else z_dn))

    def z1_copy(k, up, x):
        return rcopy(part.at[piece(k, 1 if up else 2, x)], zr1.at[k, up, x],
                     z_s, z1_r.at[k], tp_dev(z_up if up else z_dn))

    def product(q, r):
        first = (q * 4 + r) * 2
        pltpu.make_async_copy(pv.at[pl.ds(first, 2)], pv.at[pl.ds(first, 2)], pv_sem.at[q * 4 + r]).wait()

        def body(x, _):
            both = jnp.dot(sc[...], pv[(q * 4 + r) * 2 + x], preferred_element_type=F32).astype(BF16)
            part[piece(2 * q, r, x)] = both[:, :LANES]
            part[piece(2 * q + 1, r, x)] = both[:, LANES:]
            return 0

        lax.fori_loop(0, 2, body, 0)

    def z_far(k):
        z2_copy(k, 1).start()
        z2_copy(k, 0).start()

    def z_near(k, up):
        z1_copy(k, up, 1 - up).start()

    def z_middle(k):
        for up in (1, 0):
            z2_copy(k, up).wait_recv()
            u = piece(k, 1 if up else 2, up)
            part[u] = (part[u].astype(F32) + zr2[k, up].astype(F32)).astype(BF16)
            z1_copy(k, up, up).start()

    def z_total(k, x):
        return (part[piece(k, 3, x)].astype(F32) + zr1[k, 0, x].astype(F32)) + zr1[k, 1, x].astype(F32)

    def xh_copy(k):
        return rcopy(part.at[piece(k, 3, 1 - xh)], xr.at[k], z_s, xh_r.at[k], tp_dev(xh_peer))

    def z_last(k):
        arrived(zr1.at[k], z1_r.at[k])
        part[piece(k, 3, 1 - xh)] = z_total(k, 1 - xh).astype(BF16)
        xh_copy(k).start()

    def ar_copy(k, src, dst):
        return rcopy(buckets.at[k, pl.ds(pl.multiple_of((dst // 2) * 2 * CAP, 2 * CAP), 2 * CAP)],
                     arr.at[k // 2, src], ar_s, ar_r.at[k // 2], fs_dev(dst))

    def ar_mine(k):
        return pltpu.make_async_copy(
            buckets.at[k, pl.ds(pl.multiple_of(g * 2 * CAP, 2 * CAP), 2 * CAP)], arr.at[k // 2, f], my_sem.at[1 + k // 2])

    def each_owner(k, fn):
        def body(s, _):
            fn(2 * lax.rem(g + s, FS // 2) + k % 2)
            return 0

        lax.fori_loop(1, FS // 2, body, 0)

        @pl.when(c != k % 2)
        def _():
            fn(core_peer)

    def regroup(k):
        xh_copy(k).wait_recv()
        raw = z_total(k, xh) + xr[k].astype(F32)
        fitted = (raw * scale[...]).astype(BF16)
        buckets[k] = jnp.dot(onehot[...], fitted, preferred_element_type=F32).astype(BF16)
        each_owner(k, lambda d: ar_copy(k, f, d).start())

        @pl.when(c == k % 2)
        def _():
            ar_mine(k).start()

    def rs_copy(q, src, dst):
        return rcopy(pg.at[q, dst], rsv.at[q, src], rs_s.at[q], rs_r.at[2 * q + src % 2], fs_dev(dst))

    def rs_mine(q):
        return pltpu.make_async_copy(pg.at[q, f], rsv.at[q, f], my_sem.at[3 + q])

    def pair(yy, side):
        return pl.ds(pl.multiple_of(yy * 4 + side * 2, 2), 2)

    def rf_copy(q, up):
        return rcopy(pg.at[q, pair(y_far, 1 - up)], rsf.at[q, up], ry_s.at[q], rf_r.at[q, up], y_side(up))

    def ry_copy(q, up, side):
        return rcopy(pg.at[q, pair(y_up if up else y_dn, side)], rsy.at[q, up, pl.ds(side * 2, 2)],
                     ry_s.at[q], ry_r.at[q], y_side(up))

    def rs_ring(k):
        @pl.when(c == k % 2)
        def _():
            q = k // 2
            for up in (1, 0):
                rf_copy(q, up).wait_recv()
                for i in range(2):
                    at = (y_up if up else y_dn) * 4 + (1 - up) * 2 + i
                    pg[q, at] = (pg[q, at].astype(F32) + rsf[q, up, i].astype(F32)).astype(BF16)
                ry_copy(q, up, 1 - up).start()

    def rs_mid(k):
        @pl.when(c == k % 2)
        def _():
            q = k // 2
            arrived(rsy.at[q], ry_r.at[q])
            for i in range(4):
                acc = pg[q, y * 4 + i].astype(F32) + rsy[q, 0, i].astype(F32) + rsy[q, 1, i].astype(F32)
                pg[q, y * 4 + i] = acc.astype(BF16)
            for d in near_chips:
                rs_copy(q, f, d).start()
            rs_mine(q).start()

    def gradient(k, part_of):
        q = k // 2

        def one(s, total):
            src = lax.rem(f + s, FS)
            for j in range(2):
                rows = pl.ds(pl.multiple_of(j * ROWS + src * CAP, CAP), CAP)
                diff = hv[rows, q * LANES:(q + 1) * LANES] - arr[q, src, j * CAP:(j + 1) * CAP, :].astype(F32)
                wd = wcol[src, j * CAP:(j + 1) * CAP, :] * diff
                gv[rows, :] = wd * (2.0 / DENOM)
                errors = wd * diff
                for i in range(CAP // 8):
                    total = total + errors[i * 8:(i + 1) * 8]
            return total

        if part_of != 1:
            total = lb[f] if q else jnp.zeros((8, LANES), F32)
            lb[f] = lax.fori_loop(0, FS, one, total)
            if q:
                each_fs(lambda d: l1_copy(f, d).start())
            gt[...] = gv[...].T.astype(BF16)

        def term(dst):
            cols = pl.ds(pl.multiple_of(dst * KB, KB), KB)
            pg[q, dst] = jnp.dot(gt[...], cv[:, cols], preferred_element_type=F32).astype(BF16)

        def terms(yy, side):
            def one(i, _):
                term(yy * 4 + side * 2 + i)
                return 0

            lax.fori_loop(0, 2, one, 0)

        if part_of != 1:
            for up in (1, 0):
                terms(y_far, 1 - up)
                rf_copy(q, up).start()
            for up in (1, 0):
                terms(y_up if up else y_dn, up)
                ry_copy(q, up, up).start()
        if part_of != 0:
            for up in (1, 0):
                terms(y_up if up else y_dn, 1 - up)
            for side in range(2):
                terms(y, side)

    def student(k, part_of=2):
        @pl.when(c == k % 2)
        def _():
            if part_of != 1:
                ar_mine(k).wait()
                arrived(arr.at[k // 2, 0:FS - 1], ar_r.at[k // 2])
            gradient(k, part_of)

    def collect(k):
        q, h = k // 2, k % 2

        count = 2

        @pl.when(c == h)
        def _():
            rs_mine(q).wait()
            arrived(rsv.at[q, 0:count - 1], rs_r.at[k])

        @pl.when(c != h)
        def _():
            arrived(rsv.at[q, 0:count], rs_r.at[k])

        acc = rsv[q, 2 * g + h].astype(F32) + rsv[q, 2 * xl_chip + h].astype(F32)
        out_ref[q * HALF + h * LANES:q * HALF + (h + 1) * LANES, :] = acc.astype(BF16)

    def l1_copy(src, dst):
        return rcopy(lb.at[src], lb.at[src], l1_s, l1_r, fs_dev(dst))

    def l2_copy(src, dst):
        return rcopy(lt.at[src], lt.at[src], l2_s, l2_r, tp_dev(dst))

    def row_scales():
        arrived(sq.at[0:TP - 1], sq_r)
        squares = sq[0]
        for i in range(1, TP):
            squares = squares + sq[i]
        rows_scale = lax.rsqrt(squares / D_T + 1e-05)
        for i in range(4):
            scale[i * LANES:(i + 1) * LANES, :] = jnp.broadcast_to(rows_scale[i:i + 1], (LANES, LANES)).T

    def loss_a():
        arrived(lb.at[0:FS - 1], l1_r)
        total = lb[0]
        for i in range(1, FS):
            total = total + lb[i]
        lt[t] = total
        each_tp(lambda d: l2_copy(t, d).start())

    def loss_b():
        arrived(lt.at[0:TP - 1], l2_r)
        total = lt[0]
        for i in range(1, TP):
            total = total + lt[i]
        total = jnp.sum(jnp.sum(total, axis=0, keepdims=True), axis=1, keepdims=True) / DENOM
        loss_ref[...] = jnp.broadcast_to(total, (8, LANES))

    product(0, 0)
    pl.semaphore_wait(barrier, FS - 1 + TP - 1)
    z_far(0)
    wo_stage(0)
    for cp in cx:
        cp.start()
    each_tp(lambda d: sq_copy(t, d).start())
    product(0, 1)
    z_near(0, 1)
    wo_stage(1)
    product(0, 2)
    z_near(0, 0)
    z_far(1)
    each_fs(lambda d: wt_copy(f, d).start())
    product(0, 3)
    product(1, 0)
    z_middle(0)
    z_near(1, 1)
    z_near(1, 0)
    wo_stage(2)
    product(1, 1)
    product(1, 2)
    z_far(2)
    product(1, 3)
    row_scales()
    wo_stage(3)
    z_middle(1)
    z_near(2, 1)
    z_near(2, 0)
    z_far(3)
    columns_of_weights()
    z_last(0)
    hidden(0)
    wo_stage(4)
    hidden(1)
    hidden(2)
    regroup(0)
    z_middle(2)
    z_near(3, 1)
    z_near(3, 0)
    z_last(1)
    hidden(3)
    student(0, 0)
    z_middle(3)
    regroup(1)
    z_last(2)
    student(0, 1)
    rs_ring(0)
    z_last(3)
    regroup(2)
    student(1, 0)
    rs_mid(0)
    regroup(3)
    student(1, 1)
    rs_ring(1)
    student(2)
    rs_ring(2)
    student(3)
    loss_a()
    rs_mid(1)
    rs_ring(3)
    rs_mid(2)
    collect(0)
    collect(1)
    rs_mid(3)
    collect(2)
    collect(3)
    loss_b()

    sent(cv.at[0:ROWS + ROWS * HALF // D_S], core_s)
    sent(wv.at[0:15 * KB], w_s)
    sent(part.at[0:28], z_s)
    sent(arr.at[:, 0:FS - 1], ar_s)
    for q in range(2):
        sent(rsv.at[0, 0:3], rs_s.at[q])
        sent(pg.at[0, 0:12], ry_s.at[q])
    sent(wts.at[0:FS - 1], wt_s)
    sent(lb.at[0:FS - 1], l1_s)
    sent(lt.at[0:TP - 1], l2_s)
    sent(sq.at[0:TP - 1], sq_s)


def per_device(t_hid, teacher_gain, proj, owner, seg_ids, student_ctx, student_resid, w_out):
    dma = pltpu.SemaphoreType.DMA
    anyspace = pl.BlockSpec(memory_space=pl.ANY)
    vmem = pl.BlockSpec(memory_space=pltpu.VMEM)
    out, loss = pl.pallas_call(
        kernel,
        out_shape=(jax.ShapeDtypeStruct((COLS, KB), BF16), jax.ShapeDtypeStruct((8, LANES), F32)),
        in_specs=[anyspace, vmem, anyspace, vmem, vmem, anyspace, anyspace, anyspace],
        out_specs=(vmem, vmem),
        scratch_shapes=[
            pltpu.VMEM((SLAB, KT), BF16),
            pltpu.VMEM((SLAB, KT), BF16),
            pltpu.VMEM((16, KT, HALF), BF16),
            pltpu.VMEM((2 * ROWS, D_S), BF16),
            pltpu.VMEM((2, 2 * ROWS, LANES), BF16),
            pltpu.VMEM((D_S, HALF), BF16),
            pltpu.VMEM((32, SLAB, LANES), BF16),
            pltpu.VMEM((4, 2, SLAB, LANES), BF16),
            pltpu.VMEM((4, 2, 2, SLAB, LANES), BF16),
            pltpu.VMEM((4, SLAB, LANES), BF16),
            pltpu.VMEM((TP, 8, LANES), F32),
            pltpu.VMEM((SLAB, LANES), F32),
            pltpu.VMEM((ROWS, SLAB), BF16),
            pltpu.VMEM((4, ROWS, LANES), BF16),
            pltpu.VMEM((FS // 2, 8, LANES), F32),
            pltpu.VMEM((2, FS, 2 * CAP, LANES), BF16),
            pltpu.VMEM((FS, 8, LANES), F32),
            pltpu.VMEM((FS, LANES, LANES), F32),
            pltpu.VMEM((2 * ROWS, HALF), F32),
            pltpu.VMEM((2 * ROWS, LANES), F32),
            pltpu.VMEM((LANES, 2 * ROWS), BF16),
            pltpu.VMEM((2, FS, LANES, KB), BF16),
            pltpu.VMEM((2, FS, LANES, KB), BF16),
            pltpu.VMEM((2, 2, 2, LANES, KB), BF16),
            pltpu.VMEM((2, 2, 4, LANES, KB), BF16),
            pltpu.VMEM((FS, 8, LANES), F32),
            pltpu.VMEM((TP, 8, LANES), F32),
            dma((6,)), dma((8,)), dma((5,)), dma, dma, dma, dma((4,)), dma((2,)), dma, dma, dma((4,)),
            dma, dma, dma, dma, dma, dma((4, 2)), dma((4,)), dma((4,)), dma, dma((2,)), dma((2,)), dma((4,)),
            dma((2, 2)), dma((2,)), dma((2,)), dma, dma, dma, dma,
        ],
        compiler_params=pltpu.CompilerParams(collective_id=0, has_side_effects=True, vmem_limit_bytes=62 << 20),
        cost_estimate=pl.CostEstimate(flops=15 * 10 ** 9, bytes_accessed=32 << 20, transcendentals=0),
    )(t_hid, teacher_gain.reshape(1, KT), proj, owner.reshape(1, SLAB), seg_ids, student_ctx, student_resid, w_out)
    return loss[0, 0], out.T


def solution(mesh):
    return jax.shard_map(
        per_device,
        mesh=mesh,
        in_specs=(
            P("fsdp", "tp"),
            P("tp"),
            P("tp", None),
            P("fsdp", None),
            P("fsdp", None),
            P("fsdp", None),
            P("fsdp", "tp"),
            P("fsdp", "tp"),
        ),
        out_specs=(P(), P("fsdp", "tp")),
        check_vma=False,
    )
```

```python
import jax
import jax.numpy as jnp
from jax import lax
from jax.experimental import pallas as pl
from jax.experimental.pallas import tpu as pltpu
from jax.sharding import PartitionSpec as P

D_T = 16384
D_S = 4096
SEGS = 8
TP = 8
FS = 16
SLAB = 512
KT = D_T // TP
COLS = D_S // TP
CAP = 48
ROWS = FS * CAP
KB = D_S // FS
HALF = COLS // 2
LANES = 128
DENOM = D_S * FS * SEGS
F32 = jnp.float32
BF16 = jnp.bfloat16
MESH = pl.DeviceIdType.MESH


def kernel(t_ref, gain_ref, proj_ref, own_ref, seg_ref, ctx_ref, resid_ref, wout_ref,
           out_ref, loss_ref,
           tv, sc, pv, cv, rv, wv, part, zr2, zr1, xr, sq, scale, onehot, buckets, bw, arr, wts, wcol,
           hv, gv, gt, pg, rsv, rsf, rsy, lb, lt,
           t_sem, ld_sem, pv_sem, my_sem, core_s, core_r, w_s, wo_r, wy_r, wf_r, wg_r, wx_r, wt_s, wt_r, sq_s, sq_r,
           z_s, z2_r, z1_r, xh_r, ar_s, ar_r, rs_s, rs_r, rf_r, ry_s, ry_r, l1_s, l1_r, l2_s, l2_r):
    def t_rows(i):
        rows = pl.ds(i * SLAB // 4, SLAB // 4)
        return pltpu.make_async_copy(t_ref.at[rows], tv.at[rows], t_sem.at[i])

    for i in range(4):
        t_rows(i).start()
    t = lax.axis_index("tp")
    f = lax.axis_index("fsdp")
    z, xh = t // 2, t % 2
    g, c = f // 2, f % 2

    def tp_dev(i):
        return (i, f)

    def fs_dev(i):
        return (t, i)

    def rcopy(src, dst, ss, rs, dev):
        return pltpu.make_async_remote_copy(src_ref=src, dst_ref=dst, send_sem=ss, recv_sem=rs,
                                            device_id=dev, device_id_type=MESH)

    def arrived(view, sem):
        rcopy(view, view, sem, sem, fs_dev(core_peer)).wait_recv()

    def sent(view, sem):
        rcopy(view, view, sem, sem, fs_dev(core_peer)).wait_send()

    z_up, z_dn = lax.rem(t + 2, TP), lax.rem(t + 6, TP)
    xh_peer = t + 1 - 2 * xh
    core_peer = f + 1 - 2 * c
    y, xl = f // 4, g % 2
    xl_chip = g + 1 - 2 * xl

    barrier = pltpu.get_barrier_semaphore()

    def greet_fs(s, _):
        pl.semaphore_signal(barrier, inc=1, device_id=fs_dev(lax.rem(f + s, FS)), device_id_type=MESH)
        return 0

    def greet_tp(s, _):
        pl.semaphore_signal(barrier, inc=1, device_id=tp_dev(lax.rem(t + s, TP)), device_id_type=MESH)
        return 0

    lax.fori_loop(1, FS, greet_fs, 0)
    lax.fori_loop(1, TP, greet_tp, 0)

    rels = (2, 1, 3, 0)

    def unit_copy(q, r, x):
        dest = lax.rem(z + rels[r], 4) * 2 + x
        col = pl.multiple_of(dest * COLS + q * HALF, HALF)
        u = (q * 4 + r) * 2 + x
        return pltpu.make_async_copy(proj_ref.at[:, pl.ds(col, HALF)], pv.at[u], pv_sem.at[q * 4 + r])

    for x in range(2):
        unit_copy(0, 0, x).start()
    my_rows = pl.ds(pl.multiple_of(c * ROWS, ROWS), ROWS)
    ld_c = pltpu.make_async_copy(ctx_ref, cv.at[my_rows], ld_sem.at[1])
    ld_r, ld_w = [], []
    for q in range(2):
        mine = pl.ds(pl.multiple_of(q * HALF + c * LANES, LANES), LANES)
        ld_r.append(pltpu.make_async_copy(resid_ref.at[:, mine], rv.at[q, my_rows], ld_sem.at[2 + q]))
        ld_w.append(pltpu.make_async_copy(
            wout_ref.at[:, mine], wv.at[pl.ds(pl.multiple_of(f * KB, KB), KB), pl.ds(q * LANES, LANES)],
            ld_sem.at[4 + q]))
    def scale_step(i, _):
        rows = pl.ds(pl.multiple_of(i * 64, 64), 64)
        wide = tv[rows, :].astype(F32)
        sc[rows, :] = (wide * gain_ref[...]).astype(BF16)
        two = wide * wide
        acc = two[:, 0:LANES]
        for k in range(1, KT // LANES):
            acc = acc + two[:, k * LANES:(k + 1) * LANES]
        scale[rows, :] = acc
        return 0

    for i in range(4):
        t_rows(i).wait()
        if i == 3:
            for q in range(2):
                for r in range(4):
                    for x in range(2):
                        if q or r:
                            unit_copy(q, r, x).start()
            for cp in ld_w + ld_r + [ld_c]:
                cp.start()
        lax.fori_loop(2 * i, 2 * i + 2, scale_step, 0)
    row = jnp.sum(scale[...].T, axis=0, keepdims=True)
    sq[t] = jnp.concatenate([row[:, i * LANES:(i + 1) * LANES] for i in range(4)] * 2, axis=0)

    other = 1 - c
    cx = [rcopy(ctx_ref, cv.at[my_rows], core_s, core_r, fs_dev(core_peer))]
    for q in range(2):
        theirs = pl.ds(pl.multiple_of(q * HALF + other * LANES, LANES), LANES)
        cx.append(rcopy(resid_ref.at[:, theirs], rv.at[q, my_rows], core_s, core_r, fs_dev(core_peer)))

    def wo_copy(q, src, dst, lane):
        lanes = pl.ds(pl.multiple_of(q * HALF + (dst % 2) * LANES, LANES), LANES)
        return rcopy(wout_ref.at[:, lanes],
                     wv.at[pl.ds(pl.multiple_of(src * KB, KB), KB), pl.ds(q * LANES, LANES)],
                     w_s, wo_r.at[lane], fs_dev(dst))

    def wt_copy(src, dst):
        return rcopy(bw.at[dst // 2], wts.at[src],
                     wt_s, wt_r, fs_dev(dst))

    def sq_copy(src, dst):
        return rcopy(sq.at[src], sq.at[src], sq_s, sq_r, tp_dev(dst))

    def each_fs(fn):
        def body(s, _):
            fn(lax.rem(f + s, FS))
            return 0
        lax.fori_loop(1, FS, body, 0)

    def each_tp(fn):
        def body(s, _):
            fn(lax.rem(t + s, TP))
            return 0
        lax.fori_loop(1, TP, body, 0)

    wt_mine = pltpu.make_async_copy(bw.at[g], wts.at[f], my_sem.at[0])

    near_chips = (core_peer, 2 * xl_chip, 2 * xl_chip + 1)

    def w_rows(yy):
        return pl.ds(pl.multiple_of(yy * 4 * KB, 4 * KB), 4 * KB)

    y_up, y_dn, y_far = lax.rem(y + 1, 4), lax.rem(y + 3, 4), lax.rem(y + 2, 4)

    def y_dev(yy):
        return fs_dev(yy * 4 + xl * 2 + c)

    def y_side(up):
        return y_dev(y_up if up else y_dn)

    def wy_copy(up, rows):
        view = wv.at[rows, 0:LANES]
        return rcopy(view, view, w_s, wy_r.at[up], y_side(up))

    def wf_copy(up, yy):
        view = wv.at[pl.ds(pl.multiple_of(yy * 4 * KB + (0 if up else 2 * KB), 2 * KB), 2 * KB), 0:LANES]
        return rcopy(view, view, w_s, wf_r, y_side(up))

    def wg_copy(up, yy):
        src = yy * 4 + xl * 2 + (0 if up else 1)
        view = wv.at[pl.ds(pl.multiple_of(src * KB, KB), KB), LANES:HALF]
        return rcopy(view, view, w_s, wg_r, y_side(up))

    def wx_copy(yy, side):
        view = wv.at[pl.ds(pl.multiple_of((yy * 2 + side) * 2 * KB, 2 * KB), 2 * KB), LANES:HALF]
        return rcopy(view, view, w_s, wx_r.at[yy], fs_dev(2 * xl_chip + c))

    def y_cores(yy):
        return (yy * 4 + xl * 2, yy * 4 + xl * 2 + 1)

    def wo_stage(n):
        if n == 0:
            wo_copy(1, f, core_peer, 0).start()
            for d in y_cores(y_up):
                wo_copy(1, f, d, 1).start()
            for d in y_cores(y_dn):
                wo_copy(1, f, d, 2).start()
            for d in near_chips:
                wo_copy(0, f, d, 3).start()
        elif n == 1:
            ld_w[1].wait()
            wo_copy(1, core_peer, f, 0).wait_recv()
            wx_copy(y, xl).start()
        elif n == 2:
            for up, yy in ((1, y_dn), (0, y_up)):
                arrived(wv.at[0:2 * KB, LANES:HALF], wo_r.at[2 - up])
                wg_copy(up, yy).start()
                wx_copy(yy, xl).start()
            ld_w[0].wait()
            arrived(wv.at[0:3 * KB, 0:LANES], wo_r.at[3])
            wy_copy(1, w_rows(y)).start()
            wy_copy(0, w_rows(y)).start()
        elif n == 3:
            arrived(wv.at[0:2 * KB, LANES:HALF], wg_r)
            wx_copy(y_far, xl).start()
        else:
            wy_copy(1, w_rows(y_dn)).wait_recv()
            wf_copy(1, y_dn).start()
            wy_copy(0, w_rows(y_up)).wait_recv()
            wf_copy(0, y_up).start()

    def hidden(n):
        yy = (y, y_dn, y_up, y_far)[n]
        if n == 0:
            ld_c.wait()
            for cp in ld_r:
                cp.wait()
            arrived(cv.at[0:ROWS + ROWS * HALF // D_S], core_r)
        if n == 3:
            arrived(wv.at[0:4 * KB, 0:LANES], wf_r)
        wx_copy(yy, 1 - xl).wait_recv()

        def step(i, _):
            rows = pl.ds(pl.multiple_of(i * 512, 512), 512)
            depth = pl.ds(pl.multiple_of(yy * 4 * KB, 4 * KB), 4 * KB)
            prod = jnp.dot(cv[rows, depth], wv[w_rows(yy), :], preferred_element_type=F32)
            if n == 0:
                before = jnp.concatenate([rv[0, rows, :].astype(F32), rv[1, rows, :].astype(F32)], axis=1)
            else:
                before = hv[rows, :]
            hv[rows, :] = prod + before
            return 0

        lax.fori_loop(0, 2 * ROWS // 512, step, 0)

    def columns_of_weights():
        arrived(wts.at[0:FS - 1], wt_r)
        wt_mine.wait()

        def one(i, _):
            wcol[i] = jnp.broadcast_to(wts[i][0:1], (LANES, LANES)).T
            return 0

        lax.fori_loop(0, FS, one, 0)

    def piece(k, r, x):
        return (k * 4 + r) * 2 + x

    def z2_copy(k, up):
        return rcopy(part.at[piece(k, 0, up)], zr2.at[k, up], z_s, z2_r.at[k, up],
                     tp_dev(z_up if up else z_dn))

    def z1_copy(k, up, x):
        return rcopy(part.at[piece(k, 1 if up else 2, x)], zr1.at[k, up, x],
                     z_s, z1_r.at[k], tp_dev(z_up if up else z_dn))

    def product(q, r):
        first = (q * 4 + r) * 2
        pltpu.make_async_copy(pv.at[pl.ds(first, 2)], pv.at[pl.ds(first, 2)], pv_sem.at[q * 4 + r]).wait()

        def body(x, _):
            both = jnp.dot(sc[...], pv[(q * 4 + r) * 2 + x], preferred_element_type=F32).astype(BF16)
            part[piece(2 * q, r, x)] = both[:, :LANES]
            part[piece(2 * q + 1, r, x)] = both[:, LANES:]
            return 0

        lax.fori_loop(0, 2, body, 0)

    def z_far(k):
        z2_copy(k, 1).start()
        z2_copy(k, 0).start()

    def z_near(k, up):
        z1_copy(k, up, 1 - up).start()

    def z_middle(k):
        for up in (1, 0):
            z2_copy(k, up).wait_recv()
            u = piece(k, 1 if up else 2, up)
            part[u] = (part[u].astype(F32) + zr2[k, up].astype(F32)).astype(BF16)
            z1_copy(k, up, up).start()

    def z_total(k, x):
        return (part[piece(k, 3, x)].astype(F32) + zr1[k, 0, x].astype(F32)) + zr1[k, 1, x].astype(F32)

    def xh_copy(k):
        return rcopy(part.at[piece(k, 3, 1 - xh)], xr.at[k], z_s, xh_r.at[k], tp_dev(xh_peer))

    def z_last(k):
        arrived(zr1.at[k], z1_r.at[k])
        part[piece(k, 3, 1 - xh)] = z_total(k, 1 - xh).astype(BF16)
        xh_copy(k).start()

    def ar_copy(k, src, dst):
        return rcopy(buckets.at[k, pl.ds(pl.multiple_of((dst // 2) * 2 * CAP, 2 * CAP), 2 * CAP)],
                     arr.at[k // 2, src], ar_s, ar_r.at[k // 2], fs_dev(dst))

    def ar_mine(k):
        return pltpu.make_async_copy(
            buckets.at[k, pl.ds(pl.multiple_of(g * 2 * CAP, 2 * CAP), 2 * CAP)], arr.at[k // 2, f], my_sem.at[1 + k // 2])

    def each_owner(k, fn):
        def body(s, _):
            fn(2 * lax.rem(g + s, FS // 2) + k % 2)
            return 0

        lax.fori_loop(1, FS // 2, body, 0)

        @pl.when(c != k % 2)
        def _():
            fn(core_peer)

    def regroup(k):
        xh_copy(k).wait_recv()
        raw = z_total(k, xh) + xr[k].astype(F32)
        fitted = (raw * scale[...]).astype(BF16)
        buckets[k] = jnp.dot(onehot[...], fitted, preferred_element_type=F32).astype(BF16)
        each_owner(k, lambda d: ar_copy(k, f, d).start())

        @pl.when(c == k % 2)
        def _():
            ar_mine(k).start()

    def rs_copy(q, src, dst):
        return rcopy(pg.at[q, dst], rsv.at[q, src], rs_s.at[q], rs_r.at[2 * q + src % 2], fs_dev(dst))

    def rs_mine(q):
        return pltpu.make_async_copy(pg.at[q, f], rsv.at[q, f], my_sem.at[3 + q])

    def pair(yy, side):
        return pl.ds(pl.multiple_of(yy * 4 + side * 2, 2), 2)

    def rf_copy(q, up):
        return rcopy(pg.at[q, pair(y_far, 1 - up)], rsf.at[q, up], ry_s.at[q], rf_r.at[q, up], y_side(up))

    def ry_copy(q, up, side):
        return rcopy(pg.at[q, pair(y_up if up else y_dn, side)], rsy.at[q, up, pl.ds(side * 2, 2)],
                     ry_s.at[q], ry_r.at[q], y_side(up))

    def rs_ring(k):
        @pl.when(c == k % 2)
        def _():
            q = k // 2
            for up in (1, 0):
                rf_copy(q, up).wait_recv()
                for i in range(2):
                    at = (y_up if up else y_dn) * 4 + (1 - up) * 2 + i
                    pg[q, at] = (pg[q, at].astype(F32) + rsf[q, up, i].astype(F32)).astype(BF16)
                ry_copy(q, up, 1 - up).start()

    def rs_mid(k):
        @pl.when(c == k % 2)
        def _():
            q = k // 2
            arrived(rsy.at[q], ry_r.at[q])
            for i in range(4):
                acc = pg[q, y * 4 + i].astype(F32) + rsy[q, 0, i].astype(F32) + rsy[q, 1, i].astype(F32)
                pg[q, y * 4 + i] = acc.astype(BF16)
            for d in near_chips:
                rs_copy(q, f, d).start()
            rs_mine(q).start()

    def gradient(k, part_of):
        q = k // 2

        def one(s, total):
            src = lax.rem(f + s, FS)
            for j in range(2):
                rows = pl.ds(pl.multiple_of(j * ROWS + src * CAP, CAP), CAP)
                diff = hv[rows, q * LANES:(q + 1) * LANES] - arr[q, src, j * CAP:(j + 1) * CAP, :].astype(F32)
                wd = wcol[src, j * CAP:(j + 1) * CAP, :] * diff
                gv[rows, :] = wd * (2.0 / DENOM)
                errors = wd * diff
                for i in range(CAP // 8):
                    total = total + errors[i * 8:(i + 1) * 8]
            return total

        if part_of != 1:
            total = lb[f] if q else jnp.zeros((8, LANES), F32)
            lb[f] = lax.fori_loop(0, FS, one, total)
            if q:
                each_fs(lambda d: l1_copy(f, d).start())
            gt[...] = gv[...].T.astype(BF16)

        def term(dst):
            cols = pl.ds(pl.multiple_of(dst * KB, KB), KB)
            pg[q, dst] = jnp.dot(gt[...], cv[:, cols], preferred_element_type=F32).astype(BF16)

        def terms(yy, side):
            def one(i, _):
                term(yy * 4 + side * 2 + i)
                return 0

            lax.fori_loop(0, 2, one, 0)

        if part_of != 1:
            for up in (1, 0):
                terms(y_far, 1 - up)
                rf_copy(q, up).start()
            for up in (1, 0):
                terms(y_up if up else y_dn, up)
                ry_copy(q, up, up).start()
        if part_of != 0:
            for up in (1, 0):
                terms(y_up if up else y_dn, 1 - up)
            for side in range(2):
                terms(y, side)

    def student(k, part_of=2):
        @pl.when(c == k % 2)
        def _():
            if part_of != 1:
                ar_mine(k).wait()
                arrived(arr.at[k // 2, 0:FS - 1], ar_r.at[k // 2])
            gradient(k, part_of)

    def collect(k):
        q, h = k // 2, k % 2

        count = 2

        @pl.when(c == h)
        def _():
            rs_mine(q).wait()
            arrived(rsv.at[q, 0:count - 1], rs_r.at[k])

        @pl.when(c != h)
        def _():
            arrived(rsv.at[q, 0:count], rs_r.at[k])

        acc = rsv[q, 2 * g + h].astype(F32) + rsv[q, 2 * xl_chip + h].astype(F32)
        out_ref[:, q * HALF + h * LANES:q * HALF + (h + 1) * LANES] = acc.T.astype(BF16)

    def l1_copy(src, dst):
        return rcopy(lb.at[src], lb.at[src], l1_s, l1_r, fs_dev(dst))

    def l2_copy(src, dst):
        return rcopy(lt.at[src], lt.at[src], l2_s, l2_r, tp_dev(dst))

    def slots():
        own = own_ref[...]
        seg = seg_ref[...]
        marks = (lax.broadcasted_iota(jnp.int32, (FS, SLAB), 0) == own)
        earlier = (lax.broadcasted_iota(jnp.int32, (SLAB, SLAB), 0)
                   < lax.broadcasted_iota(jnp.int32, (SLAB, SLAB), 1)).astype(F32).astype(BF16)
        marks = marks.astype(F32)
        before = jnp.dot(marks.astype(BF16), earlier, preferred_element_type=F32)
        rank = jnp.sum(before * marks, axis=0, keepdims=True).astype(jnp.int32)
        slot = own * CAP + rank
        onehot[...] = (lax.broadcasted_iota(jnp.int32, (ROWS, SLAB), 0) == slot).astype(F32).astype(BF16)
        member = (lax.broadcasted_iota(jnp.int32, (SEGS, SLAB), 0) == seg).astype(F32)
        counts = jnp.sum(member, axis=1, keepdims=True)
        length = jnp.sum(member * counts, axis=0, keepdims=True)
        weight = jnp.broadcast_to((1.0 / length).astype(BF16), (16, SLAB))
        wide_slot = (own // 2) * LANES + (own % 2) * CAP + rank
        spread = (lax.broadcasted_iota(jnp.int32, (FS // 2 * LANES, SLAB), 0) == wide_slot).astype(F32).astype(BF16)
        moved = lax.dot_general(weight, spread, (((1,), (1,)), ((), ())), preferred_element_type=F32)
        for i in range(FS // 2):
            bw[i] = moved[0:8, i * LANES:(i + 1) * LANES]
        wt_mine.start()

    def row_scales():
        arrived(sq.at[0:TP - 1], sq_r)
        squares = sq[0]
        for i in range(1, TP):
            squares = squares + sq[i]
        rows_scale = lax.rsqrt(squares / D_T + 1e-05)
        for i in range(4):
            scale[i * LANES:(i + 1) * LANES, :] = jnp.broadcast_to(rows_scale[i:i + 1], (LANES, LANES)).T

    def loss_a():
        arrived(lb.at[0:FS - 1], l1_r)
        total = lb[0]
        for i in range(1, FS):
            total = total + lb[i]
        lt[t] = total
        each_tp(lambda d: l2_copy(t, d).start())

    def loss_b():
        arrived(lt.at[0:TP - 1], l2_r)
        total = lt[0]
        for i in range(1, TP):
            total = total + lt[i]
        total = jnp.sum(jnp.sum(total, axis=0, keepdims=True), axis=1, keepdims=True) / DENOM
        loss_ref[...] = total

    product(0, 0)
    pl.semaphore_wait(barrier, FS - 1 + TP - 1)
    z_far(0)
    wo_stage(0)
    for cp in cx:
        cp.start()
    each_tp(lambda d: sq_copy(t, d).start())
    product(0, 1)
    z_near(0, 1)
    wo_stage(1)
    product(0, 2)
    z_near(0, 0)
    z_far(1)
    product(0, 3)
    product(1, 0)
    z_middle(0)
    z_near(1, 1)
    z_near(1, 0)
    wo_stage(2)
    product(1, 1)
    product(1, 2)
    z_far(2)
    product(1, 3)
    slots()
    each_fs(lambda d: wt_copy(f, d).start())
    row_scales()
    wo_stage(3)
    z_middle(1)
    z_near(2, 1)
    z_near(2, 0)
    z_far(3)
    z_last(0)
    hidden(0)
    wo_stage(4)
    hidden(1)
    hidden(2)
    regroup(0)
    z_middle(2)
    z_near(3, 1)
    z_near(3, 0)
    z_last(1)
    hidden(3)
    columns_of_weights()
    student(0, 0)
    z_middle(3)
    regroup(1)
    z_last(2)
    student(0, 1)
    rs_ring(0)
    z_last(3)
    regroup(2)
    student(1, 0)
    regroup(3)
    student(1, 1)
    rs_ring(1)
    student(2)
    rs_mid(0)
    rs_ring(2)
    student(3)
    loss_a()
    rs_mid(1)
    rs_ring(3)
    rs_mid(2)
    collect(0)
    collect(1)
    rs_mid(3)
    collect(2)
    collect(3)
    loss_b()

    sent(cv.at[0:ROWS + ROWS * HALF // D_S], core_s)
    sent(wv.at[0:15 * KB], w_s)
    sent(part.at[0:28], z_s)
    sent(arr.at[:, 0:FS - 1], ar_s)
    for q in range(2):
        sent(rsv.at[0, 0:3], rs_s.at[q])
        sent(pg.at[0, 0:12], ry_s.at[q])
    sent(wts.at[0:FS - 1], wt_s)
    sent(lb.at[0:FS - 1], l1_s)
    sent(lt.at[0:TP - 1], l2_s)
    sent(sq.at[0:TP - 1], sq_s)


def per_device(t_hid, teacher_gain, proj, owner, seg_ids, student_ctx, student_resid, w_out):
    dma = pltpu.SemaphoreType.DMA
    anyspace = pl.BlockSpec(memory_space=pl.ANY)
    vmem = pl.BlockSpec(memory_space=pltpu.VMEM)
    out, loss = pl.pallas_call(
        kernel,
        out_shape=(jax.ShapeDtypeStruct((KB, COLS), BF16), jax.ShapeDtypeStruct((1, 1), F32)),
        in_specs=[anyspace, vmem, anyspace, vmem, vmem, anyspace, anyspace, anyspace],
        out_specs=(vmem, vmem),
        scratch_shapes=[
            pltpu.VMEM((SLAB, KT), BF16),
            pltpu.VMEM((SLAB, KT), BF16),
            pltpu.VMEM((16, KT, HALF), BF16),
            pltpu.VMEM((2 * ROWS, D_S), BF16),
            pltpu.VMEM((2, 2 * ROWS, LANES), BF16),
            pltpu.VMEM((D_S, HALF), BF16),
            pltpu.VMEM((32, SLAB, LANES), BF16),
            pltpu.VMEM((4, 2, SLAB, LANES), BF16),
            pltpu.VMEM((4, 2, 2, SLAB, LANES), BF16),
            pltpu.VMEM((4, SLAB, LANES), BF16),
            pltpu.VMEM((TP, 8, LANES), F32),
            pltpu.VMEM((SLAB, LANES), F32),
            pltpu.VMEM((ROWS, SLAB), BF16),
            pltpu.VMEM((4, ROWS, LANES), BF16),
            pltpu.VMEM((FS // 2, 8, LANES), F32),
            pltpu.VMEM((2, FS, 2 * CAP, LANES), BF16),
            pltpu.VMEM((FS, 8, LANES), F32),
            pltpu.VMEM((FS, LANES, LANES), F32),
            pltpu.VMEM((2 * ROWS, HALF), F32),
            pltpu.VMEM((2 * ROWS, LANES), F32),
            pltpu.VMEM((LANES, 2 * ROWS), BF16),
            pltpu.VMEM((2, FS, LANES, KB), BF16),
            pltpu.VMEM((2, FS, LANES, KB), BF16),
            pltpu.VMEM((2, 2, 2, LANES, KB), BF16),
            pltpu.VMEM((2, 2, 4, LANES, KB), BF16),
            pltpu.VMEM((FS, 8, LANES), F32),
            pltpu.VMEM((TP, 8, LANES), F32),
            dma((4,)), dma((6,)), dma((8,)), dma((5,)), dma, dma, dma, dma((4,)), dma((2,)), dma, dma, dma((4,)),
            dma, dma, dma, dma, dma, dma((4, 2)), dma((4,)), dma((4,)), dma, dma((2,)), dma((2,)), dma((4,)),
            dma((2, 2)), dma((2,)), dma((2,)), dma, dma, dma, dma,
        ],
        compiler_params=pltpu.CompilerParams(collective_id=0, has_side_effects=True, vmem_limit_bytes=62 << 20),
        cost_estimate=pl.CostEstimate(flops=15 * 10 ** 9, bytes_accessed=32 << 20, transcendentals=0),
    )(t_hid, teacher_gain.reshape(1, KT), proj, owner.reshape(1, SLAB), seg_ids, student_ctx, student_resid, w_out)
    return loss.reshape(()), out


def solution(mesh):
    return jax.shard_map(
        per_device,
        mesh=mesh,
        in_specs=(
            P("fsdp", "tp"),
            P("tp"),
            P("tp", None),
            P("fsdp", None),
            P("fsdp", None),
            P("fsdp", None),
            P("fsdp", "tp"),
            P("fsdp", "tp"),
        ),
        out_specs=(P(), P("fsdp", "tp")),
        check_vma=False,
    )
```

```python
import jax
import jax.numpy as jnp
from jax import lax
from jax.experimental import pallas as pl
from jax.experimental.pallas import tpu as pltpu
from jax.sharding import PartitionSpec as P

D_T = 16384
D_S = 4096
SEGS = 8
TP = 8
FS = 16
SLAB = 512
KT = D_T // TP
COLS = D_S // TP
CAP = 48
ROWS = FS * CAP
KB = D_S // FS
HALF = COLS // 2
LANES = 128
DENOM = D_S * FS * SEGS
F32 = jnp.float32
BF16 = jnp.bfloat16
MESH = pl.DeviceIdType.MESH


def kernel(t_ref, gain_ref, proj_ref, own_ref, seg_ref, ctx_ref, resid_ref, wout_ref,
           out_ref, loss_ref,
           tv, sc, pv, cv, rv, wv, part, zr2, zr1, xr, sq, scale, onehot, buckets, bw, arr, wts, wcol,
           hv, gv, gt, pg, rsv, rsf, rsy, lb, lt,
           ld_sem, pv_sem, my_sem, core_s, core_r, w_s, wo_r, wy_r, wf_r, wg_r, wx_r, wt_s, wt_r, sq_s, sq_r,
           z_s, z2_r, z1_r, xh_r, ar_s, ar_r, rs_s, rs_r, rf_r, ry_s, ry_r, l1_s, l1_r, l2_s, l2_r):
    t = lax.axis_index("tp")
    f = lax.axis_index("fsdp")
    z, xh = t // 2, t % 2
    g, c = f // 2, f % 2

    def tp_dev(i):
        return (i, f)

    def fs_dev(i):
        return (t, i)

    def rcopy(src, dst, ss, rs, dev):
        return pltpu.make_async_remote_copy(src_ref=src, dst_ref=dst, send_sem=ss, recv_sem=rs,
                                            device_id=dev, device_id_type=MESH)

    def arrived(view, sem):
        rcopy(view, view, sem, sem, fs_dev(core_peer)).wait_recv()

    def sent(view, sem):
        rcopy(view, view, sem, sem, fs_dev(core_peer)).wait_send()

    z_up, z_dn = lax.rem(t + 2, TP), lax.rem(t + 6, TP)
    xh_peer = t + 1 - 2 * xh
    core_peer = f + 1 - 2 * c
    y, xl = f // 4, g % 2
    xl_chip = g + 1 - 2 * xl

    barrier = pltpu.get_barrier_semaphore()

    def greet_fs(s, _):
        pl.semaphore_signal(barrier, inc=1, device_id=fs_dev(lax.rem(f + s, FS)), device_id_type=MESH)
        return 0

    def greet_tp(s, _):
        pl.semaphore_signal(barrier, inc=1, device_id=tp_dev(lax.rem(t + s, TP)), device_id_type=MESH)
        return 0

    lax.fori_loop(1, FS, greet_fs, 0)
    lax.fori_loop(1, TP, greet_tp, 0)

    ld_t = pltpu.make_async_copy(t_ref, tv, ld_sem.at[0])
    ld_t.start()
    rels = (2, 1, 3, 0)

    def unit_copy(q, r, x):
        dest = lax.rem(z + rels[r], 4) * 2 + x
        col = pl.multiple_of(dest * COLS + q * HALF, HALF)
        u = (q * 4 + r) * 2 + x
        return pltpu.make_async_copy(proj_ref.at[:, pl.ds(col, HALF)], pv.at[u], pv_sem.at[q * 4 + r])

    for x in range(2):
        unit_copy(0, 0, x).start()
    my_rows = pl.ds(pl.multiple_of(c * ROWS, ROWS), ROWS)
    ld_c = pltpu.make_async_copy(ctx_ref, cv.at[my_rows], ld_sem.at[1])
    ld_r, ld_w = [], []
    for q in range(2):
        mine = pl.ds(pl.multiple_of(q * HALF + c * LANES, LANES), LANES)
        ld_r.append(pltpu.make_async_copy(resid_ref.at[:, mine], rv.at[q, my_rows], ld_sem.at[2 + q]))
        ld_w.append(pltpu.make_async_copy(
            wout_ref.at[:, mine], wv.at[pl.ds(pl.multiple_of(f * KB, KB), KB), pl.ds(q * LANES, LANES)],
            ld_sem.at[4 + q]))
    own = own_ref[...]
    seg = seg_ref[...]
    marks = (lax.broadcasted_iota(jnp.int32, (FS, SLAB), 0) == own)
    earlier = (lax.broadcasted_iota(jnp.int32, (SLAB, SLAB), 0)
               < lax.broadcasted_iota(jnp.int32, (SLAB, SLAB), 1)).astype(F32).astype(BF16)
    marks = marks.astype(F32)
    before = jnp.dot(marks.astype(BF16), earlier, preferred_element_type=F32)
    rank = jnp.sum(before * marks, axis=0, keepdims=True).astype(jnp.int32)
    slot = own * CAP + rank
    onehot[...] = (lax.broadcasted_iota(jnp.int32, (ROWS, SLAB), 0) == slot).astype(F32).astype(BF16)
    member = (lax.broadcasted_iota(jnp.int32, (SEGS, SLAB), 0) == seg).astype(F32)
    counts = jnp.sum(member, axis=1, keepdims=True)
    length = jnp.sum(member * counts, axis=0, keepdims=True)
    weight = jnp.broadcast_to((1.0 / length).astype(BF16), (16, SLAB))
    wide_slot = (own // 2) * LANES + (own % 2) * CAP + rank
    spread = (lax.broadcasted_iota(jnp.int32, (FS // 2 * LANES, SLAB), 0) == wide_slot).astype(F32).astype(BF16)
    moved = lax.dot_general(weight, spread, (((1,), (1,)), ((), ())), preferred_element_type=F32)
    for i in range(FS // 2):
        bw[i] = moved[0:8, i * LANES:(i + 1) * LANES]

    ld_t.wait()
    for q in range(2):
        for r in range(4):
            for x in range(2):
                if q or r:
                    unit_copy(q, r, x).start()
    for cp in ld_w + ld_r + [ld_c]:
        cp.start()

    def scale_step(i, _):
        rows = pl.ds(pl.multiple_of(i * 64, 64), 64)
        wide = tv[rows, :].astype(F32)
        sc[rows, :] = (wide * gain_ref[...]).astype(BF16)
        two = wide * wide
        acc = two[:, 0:LANES]
        for k in range(1, KT // LANES):
            acc = acc + two[:, k * LANES:(k + 1) * LANES]
        scale[rows, :] = acc
        return 0

    lax.fori_loop(0, SLAB // 64, scale_step, 0)
    row = jnp.sum(scale[...].T, axis=0, keepdims=True)
    sq[t] = jnp.concatenate([row[:, i * LANES:(i + 1) * LANES] for i in range(4)] * 2, axis=0)

    other = 1 - c
    cx = [rcopy(ctx_ref, cv.at[my_rows], core_s, core_r, fs_dev(core_peer))]
    for q in range(2):
        theirs = pl.ds(pl.multiple_of(q * HALF + other * LANES, LANES), LANES)
        cx.append(rcopy(resid_ref.at[:, theirs], rv.at[q, my_rows], core_s, core_r, fs_dev(core_peer)))

    def wo_copy(q, src, dst, lane):
        lanes = pl.ds(pl.multiple_of(q * HALF + (dst % 2) * LANES, LANES), LANES)
        return rcopy(wout_ref.at[:, lanes],
                     wv.at[pl.ds(pl.multiple_of(src * KB, KB), KB), pl.ds(q * LANES, LANES)],
                     w_s, wo_r.at[lane], fs_dev(dst))

    def wt_copy(src, dst):
        return rcopy(bw.at[dst // 2], wts.at[src],
                     wt_s, wt_r, fs_dev(dst))

    def sq_copy(src, dst):
        return rcopy(sq.at[src], sq.at[src], sq_s, sq_r, tp_dev(dst))

    def each_fs(fn):
        def body(s, _):
            fn(lax.rem(f + s, FS))
            return 0
        lax.fori_loop(1, FS, body, 0)

    def each_tp(fn):
        def body(s, _):
            fn(lax.rem(t + s, TP))
            return 0
        lax.fori_loop(1, TP, body, 0)

    wt_mine = pltpu.make_async_copy(bw.at[g], wts.at[f], my_sem.at[0])
    wt_mine.start()

    near_chips = (core_peer, 2 * xl_chip, 2 * xl_chip + 1)

    def w_rows(yy):
        return pl.ds(pl.multiple_of(yy * 4 * KB, 4 * KB), 4 * KB)

    y_up, y_dn, y_far = lax.rem(y + 1, 4), lax.rem(y + 3, 4), lax.rem(y + 2, 4)

    def y_dev(yy):
        return fs_dev(yy * 4 + xl * 2 + c)

    def y_side(up):
        return y_dev(y_up if up else y_dn)

    def wy_copy(up, rows):
        view = wv.at[rows, 0:LANES]
        return rcopy(view, view, w_s, wy_r.at[up], y_side(up))

    def wf_copy(up, yy):
        view = wv.at[pl.ds(pl.multiple_of(yy * 4 * KB + (0 if up else 2 * KB), 2 * KB), 2 * KB), 0:LANES]
        return rcopy(view, view, w_s, wf_r, y_side(up))

    def wg_copy(up, yy):
        src = yy * 4 + xl * 2 + (0 if up else 1)
        view = wv.at[pl.ds(pl.multiple_of(src * KB, KB), KB), LANES:HALF]
        return rcopy(view, view, w_s, wg_r, y_side(up))

    def wx_copy(yy, side):
        view = wv.at[pl.ds(pl.multiple_of((yy * 2 + side) * 2 * KB, 2 * KB), 2 * KB), LANES:HALF]
        return rcopy(view, view, w_s, wx_r.at[yy], fs_dev(2 * xl_chip + c))

    def y_cores(yy):
        return (yy * 4 + xl * 2, yy * 4 + xl * 2 + 1)

    def wo_stage(n):
        if n == 0:
            wo_copy(1, f, core_peer, 0).start()
            for d in y_cores(y_up):
                wo_copy(1, f, d, 1).start()
            for d in y_cores(y_dn):
                wo_copy(1, f, d, 2).start()
            for d in near_chips:
                wo_copy(0, f, d, 3).start()
        elif n == 1:
            ld_w[1].wait()
            wo_copy(1, core_peer, f, 0).wait_recv()
            wx_copy(y, xl).start()
        elif n == 2:
            for up, yy in ((1, y_dn), (0, y_up)):
                arrived(wv.at[0:2 * KB, LANES:HALF], wo_r.at[2 - up])
                wg_copy(up, yy).start()
                wx_copy(yy, xl).start()
            ld_w[0].wait()
            arrived(wv.at[0:3 * KB, 0:LANES], wo_r.at[3])
            wy_copy(1, w_rows(y)).start()
            wy_copy(0, w_rows(y)).start()
        elif n == 3:
            arrived(wv.at[0:2 * KB, LANES:HALF], wg_r)
            wx_copy(y_far, xl).start()
        else:
            wy_copy(1, w_rows(y_dn)).wait_recv()
            wf_copy(1, y_dn).start()
            wy_copy(0, w_rows(y_up)).wait_recv()
            wf_copy(0, y_up).start()

    def hidden(n):
        yy = (y, y_dn, y_up, y_far)[n]
        if n == 0:
            ld_c.wait()
            for cp in ld_r:
                cp.wait()
            arrived(cv.at[0:ROWS + ROWS * HALF // D_S], core_r)
        if n == 3:
            arrived(wv.at[0:4 * KB, 0:LANES], wf_r)
        wx_copy(yy, 1 - xl).wait_recv()

        def step(i, _):
            rows = pl.ds(pl.multiple_of(i * 512, 512), 512)
            depth = pl.ds(pl.multiple_of(yy * 4 * KB, 4 * KB), 4 * KB)
            prod = jnp.dot(cv[rows, depth], wv[w_rows(yy), :], preferred_element_type=F32)
            if n == 0:
                before = jnp.concatenate([rv[0, rows, :].astype(F32), rv[1, rows, :].astype(F32)], axis=1)
            else:
                before = hv[rows, :]
            hv[rows, :] = prod + before
            return 0

        lax.fori_loop(0, 2 * ROWS // 512, step, 0)

    def columns_of_weights():
        arrived(wts.at[0:FS - 1], wt_r)
        wt_mine.wait()

        def one(i, _):
            wcol[i] = jnp.broadcast_to(wts[i][0:1], (LANES, LANES)).T
            return 0

        lax.fori_loop(0, FS, one, 0)

    def piece(k, r, x):
        return (k * 4 + r) * 2 + x

    def z2_copy(k, up):
        return rcopy(part.at[piece(k, 0, up)], zr2.at[k, up], z_s, z2_r.at[k, up],
                     tp_dev(z_up if up else z_dn))

    def z1_copy(k, up, x):
        return rcopy(part.at[piece(k, 1 if up else 2, x)], zr1.at[k, up, x],
                     z_s, z1_r.at[k], tp_dev(z_up if up else z_dn))

    def product(q, r):
        first = (q * 4 + r) * 2
        pltpu.make_async_copy(pv.at[pl.ds(first, 2)], pv.at[pl.ds(first, 2)], pv_sem.at[q * 4 + r]).wait()

        def body(x, _):
            both = jnp.dot(sc[...], pv[(q * 4 + r) * 2 + x], preferred_element_type=F32).astype(BF16)
            part[piece(2 * q, r, x)] = both[:, :LANES]
            part[piece(2 * q + 1, r, x)] = both[:, LANES:]
            return 0

        lax.fori_loop(0, 2, body, 0)

    def z_far(k):
        z2_copy(k, 1).start()
        z2_copy(k, 0).start()

    def z_near(k, up):
        z1_copy(k, up, 1 - up).start()

    def z_middle(k):
        for up in (1, 0):
            z2_copy(k, up).wait_recv()
            u = piece(k, 1 if up else 2, up)
            part[u] = (part[u].astype(F32) + zr2[k, up].astype(F32)).astype(BF16)
            z1_copy(k, up, up).start()

    def z_total(k, x):
        return (part[piece(k, 3, x)].astype(F32) + zr1[k, 0, x].astype(F32)) + zr1[k, 1, x].astype(F32)

    def xh_copy(k):
        return rcopy(part.at[piece(k, 3, 1 - xh)], xr.at[k], z_s, xh_r.at[k], tp_dev(xh_peer))

    def z_last(k):
        arrived(zr1.at[k], z1_r.at[k])
        part[piece(k, 3, 1 - xh)] = z_total(k, 1 - xh).astype(BF16)
        xh_copy(k).start()

    def ar_copy(k, src, dst):
        return rcopy(buckets.at[k, pl.ds(pl.multiple_of((dst // 2) * 2 * CAP, 2 * CAP), 2 * CAP)],
                     arr.at[k // 2, src], ar_s, ar_r.at[k // 2], fs_dev(dst))

    def ar_mine(k):
        return pltpu.make_async_copy(
            buckets.at[k, pl.ds(pl.multiple_of(g * 2 * CAP, 2 * CAP), 2 * CAP)], arr.at[k // 2, f], my_sem.at[1 + k // 2])

    def each_owner(k, fn):
        def body(s, _):
            fn(2 * lax.rem(g + s, FS // 2) + k % 2)
            return 0

        lax.fori_loop(1, FS // 2, body, 0)

        @pl.when(c != k % 2)
        def _():
            fn(core_peer)

    def regroup(k):
        xh_copy(k).wait_recv()
        raw = z_total(k, xh) + xr[k].astype(F32)
        fitted = (raw * scale[...]).astype(BF16)
        buckets[k] = jnp.dot(onehot[...], fitted, preferred_element_type=F32).astype(BF16)
        each_owner(k, lambda d: ar_copy(k, f, d).start())

        @pl.when(c == k % 2)
        def _():
            ar_mine(k).start()

    def rs_copy(q, src, dst):
        return rcopy(pg.at[q, dst], rsv.at[q, src], rs_s.at[q], rs_r.at[2 * q + src % 2], fs_dev(dst))

    def rs_mine(q):
        return pltpu.make_async_copy(pg.at[q, f], rsv.at[q, f], my_sem.at[3 + q])

    def pair(yy, side):
        return pl.ds(pl.multiple_of(yy * 4 + side * 2, 2), 2)

    def rf_copy(q, up):
        return rcopy(pg.at[q, pair(y_far, 1 - up)], rsf.at[q, up], ry_s.at[q], rf_r.at[q, up], y_side(up))

    def ry_copy(q, up, side):
        return rcopy(pg.at[q, pair(y_up if up else y_dn, side)], rsy.at[q, up, pl.ds(side * 2, 2)],
                     ry_s.at[q], ry_r.at[q], y_side(up))

    def rs_ring(k):
        @pl.when(c == k % 2)
        def _():
            q = k // 2
            for up in (1, 0):
                rf_copy(q, up).wait_recv()
                for i in range(2):
                    at = (y_up if up else y_dn) * 4 + (1 - up) * 2 + i
                    pg[q, at] = (pg[q, at].astype(F32) + rsf[q, up, i].astype(F32)).astype(BF16)
                ry_copy(q, up, 1 - up).start()

    def rs_mid(k):
        @pl.when(c == k % 2)
        def _():
            q = k // 2
            arrived(rsy.at[q], ry_r.at[q])
            for i in range(4):
                acc = pg[q, y * 4 + i].astype(F32) + rsy[q, 0, i].astype(F32) + rsy[q, 1, i].astype(F32)
                pg[q, y * 4 + i] = acc.astype(BF16)
            for d in near_chips:
                rs_copy(q, f, d).start()
            rs_mine(q).start()

    def gradient(k, part_of):
        q = k // 2

        def one(s, total):
            src = lax.rem(f + s, FS)
            for j in range(2):
                rows = pl.ds(pl.multiple_of(j * ROWS + src * CAP, CAP), CAP)
                diff = hv[rows, q * LANES:(q + 1) * LANES] - arr[q, src, j * CAP:(j + 1) * CAP, :].astype(F32)
                wd = wcol[src, j * CAP:(j + 1) * CAP, :] * diff
                gv[rows, :] = wd * (2.0 / DENOM)
                errors = wd * diff
                for i in range(CAP // 8):
                    total = total + errors[i * 8:(i + 1) * 8]
            return total

        if part_of != 1:
            total = lb[f] if q else jnp.zeros((8, LANES), F32)
            lb[f] = lax.fori_loop(0, FS, one, total)
            if q:
                each_fs(lambda d: l1_copy(f, d).start())
            gt[...] = gv[...].T.astype(BF16)

        def terms(yy, side):
            first = yy * 4 + side * 2
            cols = pl.ds(pl.multiple_of(first * KB, 2 * KB), 2 * KB)
            both = jnp.dot(gt[...], cv[:, cols], preferred_element_type=F32).astype(BF16)
            pg[q, first] = both[:, :KB]
            pg[q, first + 1] = both[:, KB:]

        if part_of != 1:
            for up in (1, 0):
                terms(y_far, 1 - up)
                rf_copy(q, up).start()
            for up in (1, 0):
                terms(y_up if up else y_dn, up)
                ry_copy(q, up, up).start()
        if part_of != 0:
            for up in (1, 0):
                terms(y_up if up else y_dn, 1 - up)
            for side in range(2):
                terms(y, side)

    def student(k, part_of=2):
        @pl.when(c == k % 2)
        def _():
            if part_of != 1:
                ar_mine(k).wait()
                arrived(arr.at[k // 2, 0:FS - 1], ar_r.at[k // 2])
            gradient(k, part_of)

    def collect(k):
        q, h = k // 2, k % 2

        count = 2

        @pl.when(c == h)
        def _():
            rs_mine(q).wait()
            arrived(rsv.at[q, 0:count - 1], rs_r.at[k])

        @pl.when(c != h)
        def _():
            arrived(rsv.at[q, 0:count], rs_r.at[k])

        acc = rsv[q, 2 * g + h].astype(F32) + rsv[q, 2 * xl_chip + h].astype(F32)
        out_ref[q * HALF + h * LANES:q * HALF + (h + 1) * LANES, :] = acc.astype(BF16)

    def l1_copy(src, dst):
        return rcopy(lb.at[src], lb.at[src], l1_s, l1_r, fs_dev(dst))

    def l2_copy(src, dst):
        return rcopy(lt.at[src], lt.at[src], l2_s, l2_r, tp_dev(dst))

    def row_scales():
        arrived(sq.at[0:TP - 1], sq_r)
        squares = sq[0]
        for i in range(1, TP):
            squares = squares + sq[i]
        rows_scale = lax.rsqrt(squares / D_T + 1e-05)
        for i in range(4):
            scale[i * LANES:(i + 1) * LANES, :] = jnp.broadcast_to(rows_scale[i:i + 1], (LANES, LANES)).T

    def loss_a():
        arrived(lb.at[0:FS - 1], l1_r)
        total = lb[0]
        for i in range(1, FS):
            total = total + lb[i]
        lt[t] = total
        each_tp(lambda d: l2_copy(t, d).start())

    def loss_b():
        arrived(lt.at[0:TP - 1], l2_r)
        total = lt[0]
        for i in range(1, TP):
            total = total + lt[i]
        total = jnp.sum(jnp.sum(total, axis=0, keepdims=True), axis=1, keepdims=True) / DENOM
        loss_ref[...] = jnp.broadcast_to(total, (8, LANES))

    product(0, 0)
    pl.semaphore_wait(barrier, FS - 1 + TP - 1)
    z_far(0)
    wo_stage(0)
    for cp in cx:
        cp.start()
    each_tp(lambda d: sq_copy(t, d).start())
    product(0, 1)
    z_near(0, 1)
    wo_stage(1)
    product(0, 2)
    z_near(0, 0)
    z_far(1)
    each_fs(lambda d: wt_copy(f, d).start())
    product(0, 3)
    product(1, 0)
    z_middle(0)
    z_near(1, 1)
    z_near(1, 0)
    wo_stage(2)
    product(1, 1)
    product(1, 2)
    z_far(2)
    product(1, 3)
    row_scales()
    wo_stage(3)
    z_middle(1)
    z_near(2, 1)
    z_near(2, 0)
    z_far(3)
    columns_of_weights()
    z_last(0)
    hidden(0)
    wo_stage(4)
    hidden(1)
    hidden(2)
    regroup(0)
    z_middle(2)
    z_near(3, 1)
    z_near(3, 0)
    z_last(1)
    hidden(3)
    student(0, 0)
    z_middle(3)
    regroup(1)
    z_last(2)
    student(0, 1)
    rs_ring(0)
    z_last(3)
    regroup(2)
    student(1, 0)
    rs_mid(0)
    regroup(3)
    student(1, 1)
    rs_ring(1)
    student(2)
    rs_ring(2)
    student(3)
    loss_a()
    rs_mid(1)
    rs_ring(3)
    rs_mid(2)
    collect(0)
    collect(1)
    rs_mid(3)
    collect(2)
    collect(3)
    loss_b()

    sent(cv.at[0:ROWS + ROWS * HALF // D_S], core_s)
    sent(wv.at[0:15 * KB], w_s)
    sent(part.at[0:28], z_s)
    sent(arr.at[:, 0:FS - 1], ar_s)
    for q in range(2):
        sent(rsv.at[0, 0:3], rs_s.at[q])
        sent(pg.at[0, 0:12], ry_s.at[q])
    sent(wts.at[0:FS - 1], wt_s)
    sent(lb.at[0:FS - 1], l1_s)
    sent(lt.at[0:TP - 1], l2_s)
    sent(sq.at[0:TP - 1], sq_s)


def per_device(t_hid, teacher_gain, proj, owner, seg_ids, student_ctx, student_resid, w_out):
    dma = pltpu.SemaphoreType.DMA
    anyspace = pl.BlockSpec(memory_space=pl.ANY)
    vmem = pl.BlockSpec(memory_space=pltpu.VMEM)
    out, loss = pl.pallas_call(
        kernel,
        out_shape=(jax.ShapeDtypeStruct((COLS, KB), BF16), jax.ShapeDtypeStruct((8, LANES), F32)),
        in_specs=[anyspace, vmem, anyspace, vmem, vmem, anyspace, anyspace, anyspace],
        out_specs=(vmem, vmem),
        scratch_shapes=[
            pltpu.VMEM((SLAB, KT), BF16),
            pltpu.VMEM((SLAB, KT), BF16),
            pltpu.VMEM((16, KT, HALF), BF16),
            pltpu.VMEM((2 * ROWS, D_S), BF16),
            pltpu.VMEM((2, 2 * ROWS, LANES), BF16),
            pltpu.VMEM((D_S, HALF), BF16),
            pltpu.VMEM((32, SLAB, LANES), BF16),
            pltpu.VMEM((4, 2, SLAB, LANES), BF16),
            pltpu.VMEM((4, 2, 2, SLAB, LANES), BF16),
            pltpu.VMEM((4, SLAB, LANES), BF16),
            pltpu.VMEM((TP, 8, LANES), F32),
            pltpu.VMEM((SLAB, LANES), F32),
            pltpu.VMEM((ROWS, SLAB), BF16),
            pltpu.VMEM((4, ROWS, LANES), BF16),
            pltpu.VMEM((FS // 2, 8, LANES), F32),
            pltpu.VMEM((2, FS, 2 * CAP, LANES), BF16),
            pltpu.VMEM((FS, 8, LANES), F32),
            pltpu.VMEM((FS, LANES, LANES), F32),
            pltpu.VMEM((2 * ROWS, HALF), F32),
            pltpu.VMEM((2 * ROWS, LANES), F32),
            pltpu.VMEM((LANES, 2 * ROWS), BF16),
            pltpu.VMEM((2, FS, LANES, KB), BF16),
            pltpu.VMEM((2, FS, LANES, KB), BF16),
            pltpu.VMEM((2, 2, 2, LANES, KB), BF16),
            pltpu.VMEM((2, 2, 4, LANES, KB), BF16),
            pltpu.VMEM((FS, 8, LANES), F32),
            pltpu.VMEM((TP, 8, LANES), F32),
            dma((6,)), dma((8,)), dma((5,)), dma, dma, dma, dma((4,)), dma((2,)), dma, dma, dma((4,)),
            dma, dma, dma, dma, dma, dma((4, 2)), dma((4,)), dma((4,)), dma, dma((2,)), dma((2,)), dma((4,)),
            dma((2, 2)), dma((2,)), dma((2,)), dma, dma, dma, dma,
        ],
        compiler_params=pltpu.CompilerParams(collective_id=0, has_side_effects=True, vmem_limit_bytes=62 << 20),
        cost_estimate=pl.CostEstimate(flops=15 * 10 ** 9, bytes_accessed=32 << 20, transcendentals=0),
    )(t_hid, teacher_gain.reshape(1, KT), proj, owner.reshape(1, SLAB), seg_ids, student_ctx, student_resid, w_out)
    return loss[0, 0], out.T


def solution(mesh):
    return jax.shard_map(
        per_device,
        mesh=mesh,
        in_specs=(
            P("fsdp", "tp"),
            P("tp"),
            P("tp", None),
            P("fsdp", None),
            P("fsdp", None),
            P("fsdp", None),
            P("fsdp", "tp"),
            P("fsdp", "tp"),
        ),
        out_specs=(P(), P("fsdp", "tp")),
        check_vma=False,
    )
```
